32 devices in a mesh: runs: 2 (over y), ja: 16 (over z, x, core).
Axes of the slice: x: 2, y: 2, z: 4, core: 2. Of those that a mesh axis runs over, the one named last changes fastest.
Arguments:
- pos_vel: float32 [6, 32768], P(None, ('runs', 'ja')), parts along dimension 1, may hold values from -4 to 4
- acc_jerk: float32 [6, 32768], P(None, ('runs', 'ja')), parts along dimension 1, may hold values from -5 to 5
- star_mass: float32 [32768], P(('runs', 'ja')), parts along dimension 0, may hold values from 1.2207031e-05 to 0.00030517578
- step_phase: float32 [32768], P(('runs', 'ja')), parts along dimension 0, may hold values from 0.25 to 1
- step_level: int32 [32768], P(('runs', 'ja')), parts along dimension 0, may hold values from 0 to 3
- counts: int32 [32], P(('runs', 'ja')), parts along dimension 0, may hold values from 1 to 256, 2048 in all
- star_order: int32 [32, 1024], P(('runs', 'ja')), parts along dimension 0, may hold values from 0 to 1023, each once within a row
Outputs:
- new_pos_vel: float32 [6, 32768], P(None, ('runs', 'ja')), parts along dimension 1
- new_acc_jerk: float32 [6, 32768], P(None, ('runs', 'ja')), parts along dimension 1
- active_state: float32 [12, 8192], P(None, ('runs', 'ja')), parts along dimension 1
The draws below stay inside these ranges and needn't reach their ends.
There are 2 independent parts, one for each index of `runs`. The reference program is written for one: setup_inputs(seed, part) draws one part's arguments, and reference() takes and returns one part's arrays. A program takes and returns all parts, laid end to end along the dimension named above; each array names one. Nothing has to cross between parts.
Inputs may be any that keep to these rules, and one draw needn't show every extreme that they name: The counts sum to 2048; the largest is exactly 256. `star_order`: each row is a permutation of the local indices.
All inputs are finite; a program needn't handle non-finite values. No bound on the sum of `counts` on one device may be relied on, other than what follows from the above.
Results may differ from the reference program's by a relative error of at most 0.00002.
Values sent between devices are 32-bit elements; how exact they have to be, the bound alone decides.
No kernel may reach another device: no remote copies, remote signals or barrier semaphores. Data moves between devices by JAX's collectives and lax.ppermute only.
A program may use at most 64 MiB of HBM per device.

```python
import math
import jax
import jax.numpy as jnp
import numpy as np
from jax import lax

N_DEV = 1024
CAP = 256
SHARDS = 16
N = 16384
A = 2048


def set_ends(values, own_key, smallest, largest):
    spot = [jax.random.randint(jax.random.fold_in(own_key, axis), (), 0, length) for axis, length in enumerate(values.shape)]
    widest = values.shape.index(max(values.shape))
    next_to = spot[:widest] + [(spot[widest] + 1) % values.shape[widest]] + spot[widest + 1:]
    return values.at[tuple(spot)].set(smallest).at[tuple(next_to)].set(largest)


def block_levels(stream_key, shape, cuts, low, high):
    level = 1.0
    for dim, shards_of in cuts:
        heights = jax.random.uniform(jax.random.fold_in(jax.random.fold_in(stream_key, 6), dim), (shards_of,), jnp.float32, low / len(cuts), high / len(cuts))
        level = level * jnp.repeat(jnp.exp(heights), shape[dim] // shards_of).reshape((-1,) + (1,) * (len(shape) - 1 - dim))
    return level


def split_up(number_of, total, limit, lean):
    portions = [(1 << 20) // math.isqrt(rank ** lean) + 1 for rank in range(2, number_of + 1)]
    surplus, given = total - limit - (number_of - 1), [1] * (number_of - 1)
    while surplus > 0:
        free = [i for i in range(number_of - 1) if given[i] < limit]
        mass, left = sum([portions[i] for i in free]), surplus
        for i in free:
            more = min(limit - given[i], max(1, left * portions[i] // mass), surplus)
            given[i] = given[i] + more
            surplus = surplus - more
    return np.array([limit] + given)


def ragged_sizes(key, count, total, most, lean):
    if count == 2:
        one = jax.random.randint(key, (), max(1, total - most), min(most, total - 1) + 1)
        return jnp.stack([one, total - one])
    sizes = jnp.asarray(split_up(count, total, most, lean), jnp.int32)
    twos = (count - 1) // 2
    donor, sink = sizes[1:1 + 2 * twos:2], sizes[2:2 + 2 * twos:2]
    slack = jnp.minimum(donor - 1, most - sink)
    passed = jax.random.randint(jax.random.fold_in(key, 1), (twos,), 0, 1 << 20) % (slack + 1)
    sizes = sizes.at[1:1 + 2 * twos:2].set(donor - passed).at[2:2 + 2 * twos:2].set(sink + passed)
    return sizes[jax.random.permutation(jax.random.fold_in(key, 2), count)]


def normal_values(key, extent, deviation, bound, cuts=(), kind=jnp.bfloat16):
    drawn = deviation * jax.random.normal(key, extent, jnp.float32)
    if cuts:
        drawn = drawn * block_levels(key, extent, cuts, -0.22, 0.18)
    return jnp.clip(drawn, -bound, bound).astype(kind)


def setup_inputs(seed: int = 0, part: int = 0) -> dict:
    arg_keys = jax.random.split(jax.random.key(seed), 8)
    part_keys = jax.random.split(jax.random.fold_in(arg_keys[7], part), 8)
    return {
        "pos_vel": normal_values(part_keys[0], (6, N), 0.7, 4.0, ((1, 16),), jnp.float32),
        "acc_jerk": normal_values(part_keys[1], (6, N), 1.0, 5.0, ((1, 16),), jnp.float32),
        "star_mass": jnp.clip(jnp.exp(math.log(0.00030517578) - 3.218876 * jax.random.uniform(part_keys[2], (N,), jnp.float32) ** block_levels(part_keys[2], (N,), ((0, 16),), -0.2, 0.2)), 1.220703143189894e-05, 0.00030517578),
        "step_phase": jnp.clip(0.25 + 0.75 * jax.random.uniform(part_keys[3], (N,), jnp.float32) ** block_levels(part_keys[3], (N,), ((0, 16),), -0.2, 0.2), 0.25, 1.0),
        "step_level": set_ends(jax.random.randint(part_keys[4], (N,), 0, 4), jax.random.fold_in(part_keys[4], 1), 0, 3).astype(jnp.int32),
        "counts": ragged_sizes(part_keys[5], SHARDS, A, CAP, 2).astype(jnp.int32),
        "star_order": jax.vmap(lambda own: jax.random.permutation(own, N_DEV))(jax.random.split(part_keys[6], SHARDS)).reshape((SHARDS, N_DEV)).astype(jnp.int32),
    }


soft_sq = 0.01
base_step = 2.0

def predict(pos_vel, acc_jerk, age):
    half_sq = 0.5 * age * age
    sixth_cube = age * age * age / 6.0
    position = pos_vel[0:3] + age * pos_vel[3:6] + half_sq * acc_jerk[0:3] + sixth_cube * acc_jerk[3:6]
    velocity = pos_vel[3:6] + age * acc_jerk[0:3] + half_sq * acc_jerk[3:6]
    return jnp.concatenate([position, velocity], axis=0)

def pair_block(targets, sources):
    delta_x = sources[0:3, None, :] - targets[0:3, :, None]
    delta_v = sources[3:6, None, :] - targets[3:6, :, None]
    dist_sq = soft_sq + delta_x[0] * delta_x[0] + delta_x[1] * delta_x[1] + delta_x[2] * delta_x[2]
    inverse = lax.rsqrt(dist_sq)
    inverse_sq = inverse * inverse
    weight = sources[6][None, :] * inverse * inverse_sq
    radial = 3.0 * (delta_x[0] * delta_v[0] + delta_x[1] * delta_v[1] + delta_x[2] * delta_v[2]) * inverse_sq
    accel_part = lax.optimization_barrier(jnp.sum(weight[None] * delta_x, axis=2))
    jerk_part = lax.optimization_barrier(jnp.sum(weight[None] * (delta_v - radial[None] * delta_x), axis=2))
    return jnp.concatenate([accel_part, jerk_part], axis=0)

def pair_forces(targets, sources, width):
    rows = targets.shape[1]
    block = math.gcd(rows, width)
    split = targets.reshape(6, rows // block, block).transpose(1, 0, 2)
    result = lax.map(lambda part: pair_block(part, sources), split)
    return result.transpose(1, 0, 2).reshape(6, rows)

def correct(old_pv, old_aj, fresh, step_len):
    half = 0.5 * step_len
    twelfth = step_len * step_len / 12.0
    velocity = old_pv[3:6] + half * (old_aj[0:3] + fresh[0:3]) + twelfth * (old_aj[3:6] - fresh[3:6])
    position = old_pv[0:3] + half * (old_pv[3:6] + velocity) + twelfth * (old_aj[0:3] - fresh[0:3])
    return jnp.concatenate([position, velocity], axis=0)

def reference(pos_vel, acc_jerk, star_mass, step_phase, step_level, counts, star_order):
    ends = jnp.cumsum(counts).astype(jnp.int32)
    starts = (ends - counts).astype(jnp.int32)
    place = jnp.arange(A, dtype=jnp.int32)
    owner = jnp.searchsorted(ends, place, side='right').astype(jnp.int32)
    slot = (place - starts[owner]).astype(jnp.int32)
    active_ids = (owner * N_DEV + star_order[owner, slot]).astype(jnp.int32)
    step_len = base_step * jnp.exp2(-step_level.astype(jnp.float32))
    is_active = jnp.zeros((N,), jnp.float32).at[active_ids].set(1.0)
    age = step_len * jnp.where(is_active > 0.5, jnp.float32(1.0), step_phase)
    predicted = predict(pos_vel, acc_jerk, age)
    sources = jnp.concatenate([predicted, star_mass[None, :]], axis=0)
    fresh = pair_forces(predicted[:, active_ids], sources, 256)
    corrected = correct(pos_vel[:, active_ids], acc_jerk[:, active_ids], fresh, step_len[active_ids])
    slot_col = jnp.arange(SHARDS * CAP, dtype=jnp.int32)
    slot_owner = (slot_col // CAP).astype(jnp.int32)
    slot_k = (slot_col - slot_owner * CAP).astype(jnp.int32)
    slot_live = slot_k < counts[slot_owner]
    list_pos = jnp.minimum(starts[slot_owner] + slot_k, A - 1).astype(jnp.int32)
    both = jnp.concatenate([corrected, fresh], axis=0)[:, list_pos]
    active_state = jnp.where(slot_live[None, :], both, jnp.zeros_like(both))
    return (pos_vel.at[:, active_ids].set(corrected), acc_jerk.at[:, active_ids].set(fresh), active_state)
```

```python
import functools

import jax
import jax.numpy as jnp
from jax import lax
from jax.experimental import pallas as pl
from jax.experimental.pallas import tpu as pltpu
from jax.sharding import PartitionSpec as P

soft_sq = 0.01
base_step = 2.0
f32 = jnp.float32
bf16 = jnp.bfloat16

CHUNK = 256
FACTOR_ROWS = 64
PARAMS = pltpu.CompilerParams(vmem_limit_bytes=48 << 20)


def round_bf16(values):
    return values.astype(bf16).astype(f32)


def split(values, terms):
    out = []
    for _ in range(terms - 1):
        head = round_bf16(values)
        out.append(head)
        values = values - head
    return out + [round_bf16(values)]


def dot3(a, b):
    return a[0:1] * b[0:1] + a[1:2] * b[1:2] + a[2:3] * b[2:3]


def star_pieces(state):
    x, u = state[0:3], state[3:6]
    grid = jnp.floor(x * 4.0 + 0.5) * 0.25
    low = x - grid
    low1 = round_bf16(low)
    low2 = round_bf16(low - low1)
    low = low1 + low2
    return (
        grid,
        low1,
        low2,
        split(u, 3),
        split(dot3(grid, grid), 2),
        2.0 * dot3(grid, low) + dot3(low, low),
        dot3(grid + low, u),
    )


def source_factors(state):
    grid, low1, low2, (u1, u2, u3), grid_sq, rest, xu = star_pieces(state)
    one = jnp.ones_like(state[0:1])
    rows = [grid] + grid_sq + [one] * 2 + split(rest, 3) + [one] * 3
    rows += [grid] * 2 + [low1] * 3 + [low2] * 2 + [u1] * 3 + [u2] * 2 + [u3] + split(xu, 3)
    used = sum(r.shape[0] for r in rows)
    return jnp.concatenate(rows + [jnp.zeros((FACTOR_ROWS - used, state.shape[1]), f32)], axis=0)


def target_factors(state):
    grid, low1, low2, (u1, u2, u3), grid_sq, rest, xu = star_pieces(state)
    one = jnp.ones_like(state[0:1])
    z1, z3 = jnp.zeros_like(one), jnp.zeros_like(grid)
    dist = [-2.0 * grid] + [one] * 2 + grid_sq + [one] * 3 + split(rest + soft_sq, 3)
    dist += [-2.0 * low1, -2.0 * low2, -2.0 * grid, -2.0 * low1, -2.0 * low2, -2.0 * grid, -2.0 * low1]
    dist += [z3] * 6 + [z1] * 3
    radial = [-u1] + [z1] * 7 + split(xu, 3)
    radial += [-u2, -u3, -u1, -u2, z3, -u1, z3]
    radial += [-grid, -low1, -low2, -grid, -low1, -grid] + [one] * 3
    used = sum(r.shape[0] for r in dist)
    pad = [jnp.zeros((FACTOR_ROWS - used, state.shape[1]), f32)]
    return jnp.concatenate(
        [jnp.concatenate(radial + pad, axis=0), jnp.concatenate(dist + pad, axis=0)], axis=1
    )


def sum_factors(state):
    mass = state[6:7]
    mass_x, mass_u = mass * state[0:3], mass * state[3:6]
    by_weight = jnp.concatenate([mass_x, mass_u, mass, jnp.zeros_like(mass)], axis=0)
    by_radial = jnp.concatenate(
        [jnp.zeros_like(mass_x), -3.0 * mass_x, jnp.zeros_like(mass), 3.0 * mass], axis=0
    )
    return (
        jnp.concatenate(split(by_weight, 3), axis=0).astype(bf16),
        jnp.concatenate(split(by_radial, 3), axis=0).astype(bf16),
    )


def add_pairs(state, factors_t, acc_ref, products, weights):
    slots = factors_t.shape[1] // 2
    chunks = state.shape[1] // CHUNK
    factors_s = source_factors(state).T.astype(bf16)
    by_weight, by_radial = sum_factors(state)

    def multiply(c):
        products[c][...] = jnp.dot(
            factors_s[c * CHUNK : (c + 1) * CHUNK], factors_t, preferred_element_type=f32
        )

    def weigh(c):
        for g in range(0, CHUNK, 16):
            for lane in range(0, slots, 128):
                cols = slice(lane, lane + 128)
                radial = products[c][g : g + 16, cols]
                dist_sq = products[c][g : g + 16, slots + lane : slots + lane + 128]
                inverse = lax.rsqrt(dist_sq)
                inverse_sq = inverse * inverse
                weight = inverse * inverse_sq
                radial = weight * (inverse_sq * radial)
                weight_hi, radial_hi = weight.astype(bf16), radial.astype(bf16)
                weights[c][g : g + 16, cols] = weight_hi
                weights[c][CHUNK + g : CHUNK + g + 16, cols] = (weight - weight_hi.astype(f32)).astype(bf16)
                weights[c][2 * CHUNK + g : 2 * CHUNK + g + 16, cols] = radial_hi
                weights[c][3 * CHUNK + g : 3 * CHUNK + g + 16, cols] = (radial - radial_hi.astype(f32)).astype(bf16)

    def total(c):
        span = slice(c * CHUNK, (c + 1) * CHUNK)
        left = [by_weight[:, span]] * 2 + [by_radial[:, span]] * 2
        acc_ref[...] += jnp.dot(jnp.concatenate(left, axis=1), weights[c][...], preferred_element_type=f32)

    multiply(0)
    for c in range(chunks):
        if c + 1 < chunks:
            multiply(c + 1)
        weigh(c)
        if c > 0:
            total(c - 1)
    total(chunks - 1)


def add_blocks(sources_ref, factors_t, acc_ref, products, weights):
    blocks = sources_ref.shape[0] // 8
    together = 2 if blocks % 2 == 0 else 1

    def step(i, _):
        rows = [sources_ref[pl.ds(pl.multiple_of((i * together + b) * 8, 8), 8), :] for b in range(together)]
        add_pairs(jnp.concatenate(rows, axis=1), factors_t, acc_ref, products, weights)
        return 0

    if blocks == together:
        step(0, 0)
    else:
        lax.fori_loop(0, blocks // together, step, 0)


def pair_scratch(blocks, stars, slots):
    chunks = stars * (2 if blocks % 2 == 0 else 1) // CHUNK
    return [pltpu.VMEM((CHUNK, 2 * slots), f32)] * chunks + [pltpu.VMEM((4 * CHUNK, slots), bf16)] * chunks


def one_hot(order_ref, stars, slots):
    row = lax.broadcasted_iota(jnp.int32, (stars, slots), 0)
    return jnp.where(row == order_ref[0:1, 0:slots], 1.0, 0.0).astype(f32).astype(bf16)


def live_slots(count_ref, slots):
    return jnp.where(lax.broadcasted_iota(jnp.int32, (1, slots), 1) < count_ref[0], 1.0, 0.0)


def spread(hot, live):
    rows = jnp.broadcast_to(live, (16, live.shape[1])).astype(bf16)
    return lax.dot_general(rows, hot, (((1,), (1,)), ((), ())), preferred_element_type=f32)[0:1]


def exact_product(rows, hot, contract):
    height = rows.shape[0]
    terms = jnp.concatenate(split(rows, 3), axis=0).astype(bf16)
    out = lax.dot_general(terms, hot, (((1,), (contract,)), ((), ())), preferred_element_type=f32)
    return out[0:height] + out[height : 2 * height] + out[2 * height : 3 * height]


def prepare_kernel(slots, count_ref, pv_ref, aj_ref, mass_ref, phase_ref, level_ref, order_ref, src_ref, old_ref, fac_ref):
    stars = pv_ref.shape[1]
    hot = one_hot(order_ref, stars, slots)
    active = spread(hot, live_slots(count_ref, slots))
    level = level_ref[...]
    step_len = base_step * jnp.where((level & 1) > 0, 0.5, 1.0) * jnp.where((level & 2) > 0, 0.25, 1.0)
    age = step_len * jnp.where(active > 0.5, 1.0, phase_ref[...])
    half_sq = 0.5 * age * age
    sixth_cube = age * age * age / 6.0
    x, v, a, j = pv_ref[0:3], pv_ref[3:6], aj_ref[0:3], aj_ref[3:6]
    position = x + age * v + half_sq * a + sixth_cube * j
    velocity = v + age * a + half_sq * j
    src_ref[...] = jnp.concatenate([position, velocity, mass_ref[...], step_len], axis=0)
    rows = jnp.concatenate([position, velocity, step_len, jnp.zeros_like(step_len), x, v, a, j, x, a[0:1]], axis=0)
    old = exact_product(rows[0:24], hot, 0)
    old_ref[...] = old
    fac_ref[...] = target_factors(old[0:8]).astype(bf16)


def pair_kernel(fresh, src_ref, fac_ref, *refs):
    if fresh:
        out_ref, acc_ref, *scratch = refs
        acc_ref[...] = jnp.zeros_like(acc_ref)
    else:
        in_ref, out_ref, acc_ref, *scratch = refs
        acc_ref[...] = in_ref[...]
    half = len(scratch) // 2
    add_blocks(src_ref, fac_ref[...], acc_ref, scratch[:half], scratch[half:])
    out_ref[...] = acc_ref[...]


def finish_kernel(count_ref, src_ref, fac_ref, in_ref, old_ref, order_ref, pv_ref, aj_ref, new_pv_ref, new_aj_ref, state_ref, acc_ref, *scratch):
    stars, slots = pv_ref.shape[1], in_ref.shape[1]
    acc_ref[...] = in_ref[...]
    half = len(scratch) // 2
    add_blocks(src_ref, fac_ref[...], acc_ref, scratch[:half], scratch[half:])
    sums = acc_ref[0:8] + acc_ref[8:16] + acc_ref[16:24]
    here, there = old_ref[0:3], old_ref[3:6]
    a1 = sums[0:3] - here * sums[6:7]
    j1 = sums[3:6] - there * sums[6:7] + here * sums[7:8]
    step_len = old_ref[6:7]
    x0, v0, a0, j0 = old_ref[8:11], old_ref[11:14], old_ref[14:17], old_ref[17:20]
    half_step = 0.5 * step_len
    twelfth = step_len * step_len / 12.0
    v1 = v0 + half_step * (a0 + a1) + twelfth * (j0 - j1)
    x1 = x0 + half_step * (v0 + v1) + twelfth * (a0 - a1)
    live = live_slots(count_ref, slots)
    state = jnp.where(live > 0.5, jnp.concatenate([x1, v1, a1, j1], axis=0), 0.0)
    state_ref[...] = state
    hot = one_hot(order_ref, stars, slots)
    rows = jnp.concatenate([state, jnp.broadcast_to(live, (4, slots))], axis=0)
    moved = exact_product(rows, hot, 1)
    active = moved[12:13] > 0.5
    new_pv_ref[...] = jnp.where(active, moved[0:6], pv_ref[...])
    new_aj_ref[...] = jnp.where(active, moved[6:12], aj_ref[...])


VMEM = pl.BlockSpec(memory_space=pltpu.VMEM)
SMEM = pl.BlockSpec(memory_space=pltpu.SMEM)


def cost(blocks, stars, slots):
    pairs = blocks * stars * slots
    return pl.CostEstimate(flops=2 * 256 * 6 * pairs, bytes_accessed=64 * blocks * stars, transcendentals=pairs)


def call_pairs(sources, factors, acc):
    blocks, stars, slots = sources.shape[0] // 8, sources.shape[1], factors.shape[1] // 2
    operands = [sources, factors] + ([] if acc is None else [acc])
    return pl.pallas_call(
        functools.partial(pair_kernel, acc is None),
        out_shape=jax.ShapeDtypeStruct((24, slots), f32),
        in_specs=[VMEM] * len(operands),
        out_specs=VMEM,
        scratch_shapes=[pltpu.VMEM((24, slots), f32)] + pair_scratch(blocks, stars, slots),
        compiler_params=PARAMS,
        cost_estimate=cost(blocks, stars, slots),
        name="pairs_%d" % blocks,
    )(*operands)


def per_device(n, slots, pos_vel, acc_jerk, star_mass, step_phase, step_level, counts, star_order):
    stars = pos_vel.shape[1]
    row = lambda values: values.reshape(1, stars)
    own, old, factors = pl.pallas_call(
        functools.partial(prepare_kernel, slots),
        out_shape=(
            jax.ShapeDtypeStruct((8, stars), f32),
            jax.ShapeDtypeStruct((24, slots), f32),
            jax.ShapeDtypeStruct((FACTOR_ROWS, 2 * slots), bf16),
        ),
        in_specs=[SMEM] + [VMEM] * 6,
        out_specs=(VMEM,) * 3,
        compiler_params=PARAMS,
        name="prepare",
    )(counts, pos_vel, acc_jerk, row(star_mass), row(step_phase), row(step_level), star_order)

    def swap(values, bit):
        return lax.ppermute(values, "ja", [(i, i ^ bit) for i in range(n)])

    held, arrived, acc = own, own, None
    bit = n // 2
    while True:
        if bit > 1:
            coming = swap(held, bit)
        across = swap(arrived, 1)
        acc = call_pairs(arrived, factors, acc)
        if bit == 1:
            break
        acc = call_pairs(across, factors, acc)
        arrived = coming
        if bit > 2:
            held = jnp.concatenate([held, arrived], axis=0)
        bit //= 2

    blocks = across.shape[0] // 8
    return pl.pallas_call(
        finish_kernel,
        out_shape=(
            jax.ShapeDtypeStruct(pos_vel.shape, f32),
            jax.ShapeDtypeStruct(acc_jerk.shape, f32),
            jax.ShapeDtypeStruct((12, slots), f32),
        ),
        in_specs=[SMEM] + [VMEM] * 7,
        out_specs=(VMEM,) * 3,
        scratch_shapes=[pltpu.VMEM((24, slots), f32)] + pair_scratch(blocks, stars, slots),
        compiler_params=PARAMS,
        cost_estimate=cost(blocks, stars, slots),
        name="finish",
    )(counts, across, factors, acc, old, star_order, pos_vel, acc_jerk)


A_DEV = 128


def solution(mesh):
    in_specs = (
        P(None, ("runs", "ja")),
        P(None, ("runs", "ja")),
        P(("runs", "ja")),
        P(("runs", "ja")),
        P(("runs", "ja")),
        P(("runs", "ja")),
        P(("runs", "ja"), None),
    )
    out_specs = (P(None, ("runs", "ja")), P(None, ("runs", "ja")), P(None, ("runs", "ja")))
    return jax.shard_map(
        functools.partial(per_device, mesh.shape["ja"], 2 * A_DEV),
        mesh=mesh,
        in_specs=in_specs,
        out_specs=out_specs,
        check_vma=False,
    )
```

```python
import functools

import jax
import jax.numpy as jnp
from jax import lax
from jax.experimental import pallas as pl
from jax.experimental.pallas import tpu as pltpu
from jax.sharding import PartitionSpec as P

soft_sq = 0.01
base_step = 2.0
f32 = jnp.float32
bf16 = jnp.bfloat16

CHUNK = 128
TOGETHER = 4
FACTOR_ROWS = 128
PARAMS = pltpu.CompilerParams(vmem_limit_bytes=32 << 20)


def round_bf16(values):
    return values.astype(bf16).astype(f32)


def split(values, terms):
    out = []
    for _ in range(terms - 1):
        head = round_bf16(values)
        out.append(head)
        values = values - head
    return out + [round_bf16(values)]


def four_terms(state):
    grid = jnp.floor(state * 4.0 + 0.5) * 0.25
    low = state - grid
    low1, low2, low3 = split(low, 3)
    return grid, low1, low2, low3, low


def row_index(state):
    return lax.broadcasted_iota(jnp.int32, state.shape, 0)


def down3(state):
    return jnp.concatenate([state[5:8], state[0:5]], axis=0)


def source_factors(state):
    row = row_index(state)
    grid, low1, low2, low3, low = four_terms(state)
    square = jnp.where(row == 6, 1.0, grid * grid)
    rest = jnp.where(row < 3, (2.0 * grid + low) * low, (grid + low) * down3(grid + low))
    rest1, rest2, rest3 = [jnp.where(row == 6, 1.0, term) for term in split(rest, 3)]
    square1 = round_bf16(square)
    square2 = jnp.where(row == 6, 1.0, square - square1)
    groups = [grid, square1, square2, grid, grid, grid, low1, low1, low1, low2, low2, low3, rest1, rest2, rest3]
    pad = [jnp.zeros_like(state)] * (FACTOR_ROWS // 8 - len(groups))
    return jnp.concatenate(groups + pad, axis=0).astype(bf16)


def target_factors(state):
    grid, low1, low2, low3, low = four_terms(state)
    zero, one = jnp.zeros_like(state), jnp.ones_like(state)
    z1, z2, z3 = zero[0:1], zero[0:2], zero[0:3]

    def add3(values):
        return values[0:1] + values[1:2] + values[2:3]

    def near(values):
        return jnp.concatenate([-2.0 * values[0:3], z3, z2], axis=0)

    def crossed(values):
        return jnp.concatenate([-values[3:6], -values[0:3], z2], axis=0)

    def sums(first, second, scalar):
        return jnp.concatenate([first, second, scalar, z1], axis=0)

    square1, square2 = split(add3(grid[0:3] * grid[0:3]), 2)
    rest = split(add3((2.0 * grid[0:3] + low[0:3]) * low[0:3]) + soft_sq, 3)
    moved = split(add3((grid + low)[0:3] * (grid + low)[3:6]), 3)
    o3 = one[0:3]
    dist = [near(grid), sums(o3, z3, square1), sums(o3, z3, square2), near(low1), near(low2), near(low3)]
    dist += [near(grid), near(low1), near(low2), near(grid), near(low1), near(grid)]
    dist += [sums(o3, z3, term) for term in rest]
    radial = [crossed(grid), zero, zero, crossed(low1), crossed(low2), crossed(low3)]
    radial += [crossed(grid), crossed(low1), crossed(low2), crossed(grid), crossed(low1), crossed(grid)]
    radial += [sums(z3, o3, term) for term in moved]
    pad = [zero] * (FACTOR_ROWS // 8 - len(dist))
    return jnp.concatenate(
        [jnp.concatenate(radial + pad, axis=0), jnp.concatenate(dist + pad, axis=0)], axis=1
    ).astype(bf16)


def sum_factors(state):
    row = row_index(state)
    mass = jnp.broadcast_to(state[6:7], state.shape)
    by_weight = mass * jnp.where(row < 6, state, jnp.where(row == 6, 1.0, 0.0))
    by_radial = mass * jnp.where(row < 3, 0.0, jnp.where(row < 6, -3.0 * down3(state), jnp.where(row == 7, 3.0, 0.0)))
    return (
        jnp.concatenate(split(by_weight, 3), axis=0).astype(bf16),
        jnp.concatenate(split(by_radial, 3), axis=0).astype(bf16),
    )


def add_pairs(states, factors_t, acc_ref, products, weights):
    slots = factors_t.shape[1] // 2
    per = states[0].shape[1] // CHUNK
    ready = {}

    def prepare(b):
        ready[b] = (source_factors(states[b]).T,) + sum_factors(states[b])

    def span(c):
        return slice(c % per * CHUNK, (c % per + 1) * CHUNK)

    def multiply(c):
        products[c][...] = jnp.dot(ready[c // per][0][span(c)], factors_t, preferred_element_type=f32)

    def weigh(c):
        for g in range(0, CHUNK, 16):
            for lane in range(0, slots, 128):
                cols = slice(lane, lane + 128)
                radial = products[c][g : g + 16, cols]
                dist_sq = products[c][g : g + 16, slots + lane : slots + lane + 128]
                inverse = lax.rsqrt(dist_sq)
                inverse_sq = inverse * inverse
                weight = inverse * inverse_sq
                radial = weight * (inverse_sq * radial)
                weight_hi, radial_hi = weight.astype(bf16), radial.astype(bf16)
                weights[c][g : g + 16, cols] = weight_hi
                weights[c][CHUNK + g : CHUNK + g + 16, cols] = (weight - weight_hi.astype(f32)).astype(bf16)
                weights[c][2 * CHUNK + g : 2 * CHUNK + g + 16, cols] = radial_hi
                weights[c][3 * CHUNK + g : 3 * CHUNK + g + 16, cols] = (radial - radial_hi.astype(f32)).astype(bf16)

    def total(c):
        _, by_weight, by_radial = ready[c // per]
        left = [by_weight[:, span(c)]] * 2 + [by_radial[:, span(c)]] * 2
        acc_ref[...] += jnp.dot(jnp.concatenate(left, axis=1), weights[c][...], preferred_element_type=f32)

    chunks = len(states) * per
    prepare(0)
    multiply(0)
    for c in range(chunks):
        if (c + 2) % per == 0 and (c + 2) // per < len(states):
            prepare((c + 2) // per)
        if c + 1 < chunks:
            multiply(c + 1)
        weigh(c)
        if c > 0:
            total(c - 1)
    total(chunks - 1)


def blocks_together(blocks):
    return next(t for t in range(TOGETHER, 0, -1) if blocks % t == 0)


def add_blocks(sources_ref, factors_t, acc_ref, products, weights):
    blocks = sources_ref.shape[0] // 8
    together = blocks_together(blocks)

    def step(i, _):
        rows = [sources_ref[pl.ds(pl.multiple_of((i * together + b) * 8, 8), 8), :] for b in range(together)]
        add_pairs(rows, factors_t, acc_ref, products, weights)
        return 0

    if blocks == together:
        step(0, 0)
    else:
        lax.fori_loop(0, blocks // together, step, 0)


def pair_scratch(blocks, stars, slots):
    chunks = stars * blocks_together(blocks) // CHUNK
    return [pltpu.VMEM((CHUNK, 2 * slots), f32)] * chunks + [pltpu.VMEM((4 * CHUNK, slots), bf16)] * chunks


def one_hot(order_ref, stars, slots):
    row = lax.broadcasted_iota(jnp.int32, (stars, slots), 0)
    return jnp.where(row == order_ref[0:1, 0:slots], 1.0, 0.0).astype(f32).astype(bf16)


def live_slots(count_ref, slots):
    return jnp.where(lax.broadcasted_iota(jnp.int32, (1, slots), 1) < count_ref[0], 1.0, 0.0)


def spread(hot, live):
    rows = jnp.broadcast_to(live, (16, live.shape[1])).astype(bf16)
    return lax.dot_general(rows, hot, (((1,), (1,)), ((), ())), preferred_element_type=f32)[0:1]


def exact_product(rows, hot, contract):
    height = rows.shape[0]
    terms = jnp.concatenate(split(rows, 3), axis=0).astype(bf16)
    out = lax.dot_general(terms, hot, (((1,), (contract,)), ((), ())), preferred_element_type=f32)
    return out[0:height] + out[height : 2 * height] + out[2 * height : 3 * height]


def fetch(pairs, sems):
    copies = [pltpu.make_async_copy(src, dst, sems.at[i]) for i, (src, dst) in enumerate(pairs)]
    for copy in copies:
        copy.start()

    def wait(*places):
        for i in places:
            copies[i].wait()

    return wait


def prepare_kernel(slots, count_hbm, pv_hbm, aj_hbm, mass_hbm, phase_hbm, level_hbm, order_hbm, src_ref, old_ref, fac_ref, count_ref, pv_ref, aj_ref, mass_ref, phase_ref, level_ref, order_ref, sems):
    hbm = (order_hbm, count_hbm, phase_hbm, level_hbm, mass_hbm, pv_hbm, aj_hbm)
    here = (order_ref, count_ref, phase_ref, level_ref, mass_ref, pv_ref, aj_ref)
    wait = fetch(tuple(zip(hbm, here)), sems)
    stars = pv_ref.shape[1]
    wait(0, 1)
    hot = one_hot(order_ref, stars, slots)
    active = spread(hot, live_slots(count_ref, slots))
    wait(2, 3, 4, 5, 6)
    level = level_ref[...]
    step_len = base_step * jnp.where((level & 1) > 0, 0.5, 1.0) * jnp.where((level & 2) > 0, 0.25, 1.0)
    age = step_len * jnp.where(active > 0.5, 1.0, phase_ref[...])
    half_sq = 0.5 * age * age
    sixth_cube = age * age * age / 6.0
    pv, aj = pv_ref[...], aj_ref[...]
    x, v, a, j = pv[0:3], pv[3:6], aj[0:3], aj[3:6]
    position = x + age * v + half_sq * a + sixth_cube * j
    velocity = v + age * a + half_sq * j
    state = jnp.concatenate([position, velocity, mass_ref[...], step_len], axis=0)
    src_ref[...] = state
    gap = jnp.zeros((2, stars), f32)
    old = exact_product(jnp.concatenate([state, pv, gap, aj, gap], axis=0), hot, 0)
    old_ref[...] = old
    fac_ref[...] = target_factors(old[0:8])


def pair_kernel(fresh, src_ref, fac_ref, *refs):
    if fresh:
        out_ref, acc_ref, *scratch = refs
        acc_ref[...] = jnp.zeros_like(acc_ref)
    else:
        in_ref, out_ref, acc_ref, *scratch = refs
        acc_ref[...] = in_ref[...]
    half = len(scratch) // 2
    add_blocks(src_ref, fac_ref[...], acc_ref, scratch[:half], scratch[half:])
    out_ref[...] = acc_ref[...]


def finish_kernel(count_hbm, src_ref, fac_ref, in_ref, old_ref, order_hbm, pv_hbm, aj_hbm, new_pv_ref, new_aj_ref, state_ref, count_ref, order_ref, pv_ref, aj_ref, sems, acc_ref, *scratch):
    wait = fetch(((count_hbm, count_ref), (order_hbm, order_ref), (pv_hbm, pv_ref), (aj_hbm, aj_ref)), sems)
    stars, slots = pv_ref.shape[1], in_ref.shape[1]
    acc_ref[...] = in_ref[...]
    half = len(scratch) // 2
    add_blocks(src_ref, fac_ref[...], acc_ref, scratch[:half], scratch[half:])
    sums = acc_ref[0:8] + acc_ref[8:16] + acc_ref[16:24]
    old = old_ref[...]
    here, there, step_len = old[0:3], old[3:6], old[7:8]
    a1 = sums[0:3] - here * sums[6:7]
    j1 = sums[3:6] - there * sums[6:7] + here * sums[7:8]
    x0, v0, a0, j0 = old[8:11], old[11:14], old[16:19], old[19:22]
    half_step = 0.5 * step_len
    twelfth = step_len * step_len / 12.0
    v1 = v0 + half_step * (a0 + a1) + twelfth * (j0 - j1)
    x1 = x0 + half_step * (v0 + v1) + twelfth * (a0 - a1)
    wait(0, 1, 2, 3)
    live = live_slots(count_ref, slots)
    state = jnp.where(live > 0.5, jnp.concatenate([x1, v1, a1, j1], axis=0), 0.0)
    state_ref[...] = state
    hot = one_hot(order_ref, stars, slots)
    rows = jnp.concatenate([state, jnp.broadcast_to(live, (4, slots))], axis=0)
    moved = exact_product(rows, hot, 1)
    active = moved[12:13] > 0.5
    new_pv_ref[...] = jnp.where(active, moved[0:6], pv_ref[...])
    new_aj_ref[...] = jnp.where(active, moved[6:12], aj_ref[...])


VMEM = pl.BlockSpec(memory_space=pltpu.VMEM)
HBM = pl.BlockSpec(memory_space=pltpu.HBM)


def cost(blocks, stars, slots):
    pairs = blocks * stars * slots
    return pl.CostEstimate(flops=2 * 256 * 6 * pairs, bytes_accessed=64 * blocks * stars, transcendentals=pairs)


def call_pairs(sources, factors, acc):
    blocks, stars, slots = sources.shape[0] // 8, sources.shape[1], factors.shape[1] // 2
    operands = [sources, factors] + ([] if acc is None else [acc])
    return pl.pallas_call(
        functools.partial(pair_kernel, acc is None),
        out_shape=jax.ShapeDtypeStruct((24, slots), f32),
        in_specs=[VMEM] * len(operands),
        out_specs=VMEM,
        scratch_shapes=[pltpu.VMEM((24, slots), f32)] + pair_scratch(blocks, stars, slots),
        compiler_params=PARAMS,
        cost_estimate=cost(blocks, stars, slots),
        name="pairs_%d" % blocks,
    )(*operands)


def per_device(n, slots, pos_vel, acc_jerk, star_mass, step_phase, step_level, counts, star_order):
    stars = pos_vel.shape[1]
    row = lambda values: values.reshape(1, stars)
    own, old, factors = pl.pallas_call(
        functools.partial(prepare_kernel, slots),
        out_shape=(
            jax.ShapeDtypeStruct((8, stars), f32),
            jax.ShapeDtypeStruct((24, slots), f32),
            jax.ShapeDtypeStruct((FACTOR_ROWS, 2 * slots), bf16),
        ),
        in_specs=[HBM] * 7,
        out_specs=(VMEM,) * 3,
        scratch_shapes=[pltpu.SMEM((1,), jnp.int32), pltpu.VMEM(pos_vel.shape, f32), pltpu.VMEM(acc_jerk.shape, f32)]
        + [pltpu.VMEM((1, stars), f32)] * 2
        + [pltpu.VMEM((1, stars), jnp.int32)] * 2
        + [pltpu.SemaphoreType.DMA((7,))],
        compiler_params=PARAMS,
        name="prepare",
    )(counts, pos_vel, acc_jerk, row(star_mass), row(step_phase), row(step_level), star_order)

    def swap(values, bit):
        return lax.ppermute(values, "ja", [(i, i ^ bit) for i in range(n)])

    held, arrived, acc = own, own, None
    bit = n // 2
    while True:
        if bit > 1:
            coming = swap(held, bit)
        across = swap(arrived, 1)
        acc = call_pairs(arrived, factors, acc)
        if bit == 1:
            break
        acc = call_pairs(across, factors, acc)
        arrived, acc = lax.optimization_barrier((coming, acc))
        if bit > 2:
            held = jnp.concatenate([held, arrived], axis=0)
        bit //= 2

    blocks = across.shape[0] // 8
    return pl.pallas_call(
        finish_kernel,
        out_shape=(
            jax.ShapeDtypeStruct(pos_vel.shape, f32),
            jax.ShapeDtypeStruct(acc_jerk.shape, f32),
            jax.ShapeDtypeStruct((12, slots), f32),
        ),
        in_specs=[HBM] + [VMEM] * 4 + [HBM] * 3,
        out_specs=(VMEM,) * 3,
        scratch_shapes=[pltpu.SMEM((1,), jnp.int32), pltpu.VMEM((1, stars), jnp.int32)]
        + [pltpu.VMEM(pos_vel.shape, f32), pltpu.VMEM(acc_jerk.shape, f32), pltpu.SemaphoreType.DMA((4,))]
        + [pltpu.VMEM((24, slots), f32)]
        + pair_scratch(blocks, stars, slots),
        compiler_params=PARAMS,
        cost_estimate=cost(blocks, stars, slots),
        name="finish",
    )(counts, across, factors, acc, old, star_order, pos_vel, acc_jerk)


A_DEV = 128


def solution(mesh):
    in_specs = (
        P(None, ("runs", "ja")),
        P(None, ("runs", "ja")),
        P(("runs", "ja")),
        P(("runs", "ja")),
        P(("runs", "ja")),
        P(("runs", "ja")),
        P(("runs", "ja"), None),
    )
    out_specs = (P(None, ("runs", "ja")), P(None, ("runs", "ja")), P(None, ("runs", "ja")))
    return jax.shard_map(
        functools.partial(per_device, mesh.shape["ja"], 2 * A_DEV),
        mesh=mesh,
        in_specs=in_specs,
        out_specs=out_specs,
        check_vma=False,
    )
```

```python
import functools

import jax
import jax.numpy as jnp
from jax import lax
from jax.experimental import pallas as pl
from jax.experimental.pallas import tpu as pltpu
from jax.sharding import PartitionSpec as P

soft_sq = 0.01
base_step = 2.0
f32 = jnp.float32
bf16 = jnp.bfloat16

CHUNK = 128
TOGETHER = 4
FACTOR_ROWS = 128
PARAMS = pltpu.CompilerParams(vmem_limit_bytes=32 << 20)


def round_bf16(values):
    return values.astype(bf16).astype(f32)


def split(values, terms):
    out = []
    for _ in range(terms - 1):
        head = round_bf16(values)
        out.append(head)
        values = values - head
    return out + [round_bf16(values)]


def four_terms(state):
    grid = jnp.floor(state * 4.0 + 0.5) * 0.25
    low = state - grid
    low1, low2, low3 = split(low, 3)
    return grid, low1, low2, low3, low


def row_index(state):
    return lax.broadcasted_iota(jnp.int32, state.shape, 0)


def down3(state):
    return jnp.concatenate([state[5:8], state[0:5]], axis=0)


def source_factors(state):
    row = row_index(state)
    grid, low1, low2, low3, low = four_terms(state)
    square = jnp.where(row == 6, 1.0, grid * grid)
    rest = jnp.where(row < 3, (2.0 * grid + low) * low, (grid + low) * down3(grid + low))
    rest1, rest2, rest3 = [jnp.where(row == 6, 1.0, term) for term in split(rest, 3)]
    square1 = round_bf16(square)
    square2 = jnp.where(row == 6, 1.0, square - square1)
    groups = [grid, square1, square2, grid, grid, grid, low1, low1, low1, low2, low2, low3, rest1, rest2, rest3]
    pad = [jnp.zeros_like(state)] * (FACTOR_ROWS // 8 - len(groups))
    return jnp.concatenate(groups + pad, axis=0).astype(bf16)


def target_factors(state):
    grid, low1, low2, low3, low = four_terms(state)
    zero, one = jnp.zeros_like(state), jnp.ones_like(state)
    z1, z2, z3 = zero[0:1], zero[0:2], zero[0:3]

    def add3(values):
        return values[0:1] + values[1:2] + values[2:3]

    def near(values):
        return jnp.concatenate([-2.0 * values[0:3], z3, z2], axis=0)

    def crossed(values):
        return jnp.concatenate([-values[3:6], -values[0:3], z2], axis=0)

    def sums(first, second, scalar):
        return jnp.concatenate([first, second, scalar, z1], axis=0)

    square1, square2 = split(add3(grid[0:3] * grid[0:3]), 2)
    rest = split(add3((2.0 * grid[0:3] + low[0:3]) * low[0:3]) + soft_sq, 3)
    moved = split(add3((grid + low)[0:3] * (grid + low)[3:6]), 3)
    o3 = one[0:3]
    dist = [near(grid), sums(o3, z3, square1), sums(o3, z3, square2), near(low1), near(low2), near(low3)]
    dist += [near(grid), near(low1), near(low2), near(grid), near(low1), near(grid)]
    dist += [sums(o3, z3, term) for term in rest]
    radial = [crossed(grid), zero, zero, crossed(low1), crossed(low2), crossed(low3)]
    radial += [crossed(grid), crossed(low1), crossed(low2), crossed(grid), crossed(low1), crossed(grid)]
    radial += [sums(z3, o3, term) for term in moved]
    pad = [zero] * (FACTOR_ROWS // 8 - len(dist))
    return jnp.concatenate(
        [jnp.concatenate(radial + pad, axis=0), jnp.concatenate(dist + pad, axis=0)], axis=1
    ).astype(bf16)


def sum_factors(state):
    row = row_index(state)
    mass = jnp.broadcast_to(state[6:7], state.shape)
    by_weight = mass * jnp.where(row < 6, state, jnp.where(row == 6, 1.0, 0.0))
    by_radial = mass * jnp.where(row < 3, 0.0, jnp.where(row < 6, -3.0 * down3(state), jnp.where(row == 7, 3.0, 0.0)))
    return (
        jnp.concatenate(split(by_weight, 3), axis=0).astype(bf16),
        jnp.concatenate(split(by_radial, 3), axis=0).astype(bf16),
    )


def add_pairs(states, factors_t, acc_ref, products, weights):
    slots = factors_t.shape[1] // 2
    per = states[0].shape[1] // CHUNK
    ready = {}

    def prepare(b):
        ready[b] = (source_factors(states[b]).T,) + sum_factors(states[b])

    def span(c):
        return slice(c % per * CHUNK, (c % per + 1) * CHUNK)

    def multiply(c):
        products[c][...] = jnp.dot(ready[c // per][0][span(c)], factors_t, preferred_element_type=f32)

    def weigh(c):
        for g in range(0, CHUNK, 16):
            for lane in range(0, slots, 128):
                cols = slice(lane, lane + 128)
                radial = products[c][g : g + 16, cols]
                dist_sq = products[c][g : g + 16, slots + lane : slots + lane + 128]
                inverse = lax.rsqrt(dist_sq)
                inverse_sq = inverse * inverse
                weight = inverse * inverse_sq
                radial = weight * (inverse_sq * radial)
                weight_hi, radial_hi = weight.astype(bf16), radial.astype(bf16)
                weights[c][g : g + 16, cols] = weight_hi
                weights[c][CHUNK + g : CHUNK + g + 16, cols] = (weight - weight_hi.astype(f32)).astype(bf16)
                weights[c][2 * CHUNK + g : 2 * CHUNK + g + 16, cols] = radial_hi
                weights[c][3 * CHUNK + g : 3 * CHUNK + g + 16, cols] = (radial - radial_hi.astype(f32)).astype(bf16)

    def total(c):
        _, by_weight, by_radial = ready[c // per]
        left = [by_weight[:, span(c)]] * 2 + [by_radial[:, span(c)]] * 2
        acc_ref[...] += jnp.dot(jnp.concatenate(left, axis=1), weights[c][...], preferred_element_type=f32)

    chunks = len(states) * per
    prepare(0)
    multiply(0)
    for c in range(chunks):
        if (c + 2) % per == 0 and (c + 2) // per < len(states):
            prepare((c + 2) // per)
        if c + 1 < chunks:
            multiply(c + 1)
        weigh(c)
        if c > 0:
            total(c - 1)
    total(chunks - 1)


def blocks_together(shapes):
    counts = [shape[0] // 8 for shape in shapes]
    if sum(counts) <= TOGETHER:
        return sum(counts)
    return next(t for t in range(TOGETHER, 0, -1) if all(c % t == 0 for c in counts))


def add_blocks(sources, factors_t, acc_ref, scratch):
    together = blocks_together([ref.shape for ref in sources])
    products, weights = scratch[: len(scratch) // 2], scratch[len(scratch) // 2 :]

    def block(ref, b):
        return ref[pl.ds(pl.multiple_of(b * 8, 8), 8), :]

    if sum(ref.shape[0] // 8 for ref in sources) == together:
        rows = [ref[b : b + 8] for ref in sources for b in range(0, ref.shape[0], 8)]
        add_pairs(rows, factors_t, acc_ref, products, weights)
        return
    for ref in sources:

        def step(i, _):
            add_pairs([block(ref, i * together + b) for b in range(together)], factors_t, acc_ref, products, weights)
            return 0

        lax.fori_loop(0, ref.shape[0] // 8 // together, step, 0)


def pair_scratch(sources, slots):
    chunks = sources[0].shape[1] * blocks_together([s.shape for s in sources]) // CHUNK
    return [pltpu.VMEM((CHUNK, 2 * slots), f32)] * chunks + [pltpu.VMEM((4 * CHUNK, slots), bf16)] * chunks


def one_hot(order, stars):
    row = lax.broadcasted_iota(jnp.int32, (stars, order.shape[1]), 0)
    return jnp.where(row == order, 1.0, 0.0).astype(f32).astype(bf16)


def spread(hot, live):
    rows = jnp.broadcast_to(live, (16, live.shape[1])).astype(bf16)
    return lax.dot_general(rows, hot, (((1,), (1,)), ((), ())), preferred_element_type=f32)[0:1]


def exact_product(rows, hot, contract):
    height = rows.shape[0]
    terms = jnp.concatenate(split(rows, 3), axis=0).astype(bf16)
    out = lax.dot_general(terms, hot, (((1,), (contract,)), ((), ())), preferred_element_type=f32)
    return out[0:height] + out[height : 2 * height] + out[2 * height : 3 * height]


def prepare_kernel(slots, *refs):
    inputs, (src_ref, old_ref, fac_ref), here, sems = refs[:7], refs[7:10], refs[10:17], refs[17]
    copies = [pltpu.make_async_copy(src, dst, sems.at[i]) for i, (src, dst) in enumerate(zip(inputs, here))]
    for copy in copies:
        copy.start()
    pv_ref, aj_ref, mass_ref, phase_ref, level_ref, count_ref, order_ref = here
    stars = pv_ref.shape[1]
    copies[5].wait()
    copies[6].wait()
    order = order_ref[0:1, 0:slots]
    hot = one_hot(order, stars)
    live = jnp.where(lax.broadcasted_iota(jnp.int32, (1, slots), 1) < count_ref[...], 1.0, 0.0)
    active = spread(hot, live)
    for copy in copies[:5]:
        copy.wait()
    level = level_ref[...]
    step_len = base_step * jnp.where((level & 1) > 0, 0.5, 1.0) * jnp.where((level & 2) > 0, 0.25, 1.0)
    age = step_len * jnp.where(active > 0.5, 1.0, phase_ref[...])
    half_sq = 0.5 * age * age
    sixth_cube = age * age * age / 6.0
    pv, aj = pv_ref[...], aj_ref[...]
    x, v, a, j = pv[0:3], pv[3:6], aj[0:3], aj[3:6]
    position = x + age * v + half_sq * a + sixth_cube * j
    velocity = v + age * a + half_sq * j
    state = jnp.concatenate([position, velocity, mass_ref[...], step_len], axis=0)
    src_ref[...] = state
    gap = jnp.zeros((2, stars), f32)
    old = exact_product(jnp.concatenate([state, pv, gap, aj, gap], axis=0), hot, 0)
    old_ref[...] = jnp.concatenate([old[0:22], live, order.astype(f32)], axis=0)
    fac_ref[...] = target_factors(old[0:8])


def pair_kernel(parts, fresh, *refs):
    sources, fac_ref, refs = refs[:parts], refs[parts], refs[parts + 1 :]
    if fresh:
        out_ref, acc_ref, *scratch = refs
        acc_ref[...] = jnp.zeros_like(acc_ref)
    else:
        in_ref, out_ref, acc_ref, *scratch = refs
        acc_ref[...] = in_ref[...]
    add_blocks(sources, fac_ref[...], acc_ref, scratch)
    out_ref[...] = acc_ref[...]


def finish_kernel(parts, *refs):
    sources, refs = refs[:parts], refs[parts:]
    fac_ref, in_ref, old_ref, pv_ref, aj_ref, new_pv_ref, new_aj_ref, state_ref, acc_ref, *scratch = refs
    stars, slots = pv_ref.shape[1], in_ref.shape[1]
    acc_ref[...] = in_ref[...]
    add_blocks(sources, fac_ref[...], acc_ref, scratch)
    sums = acc_ref[0:8] + acc_ref[8:16] + acc_ref[16:24]
    old = old_ref[...]
    here, there, step_len = old[0:3], old[3:6], old[7:8]
    a1 = sums[0:3] - here * sums[6:7]
    j1 = sums[3:6] - there * sums[6:7] + here * sums[7:8]
    x0, v0, a0, j0 = old[8:11], old[11:14], old[16:19], old[19:22]
    half_step = 0.5 * step_len
    twelfth = step_len * step_len / 12.0
    v1 = v0 + half_step * (a0 + a1) + twelfth * (j0 - j1)
    x1 = x0 + half_step * (v0 + v1) + twelfth * (a0 - a1)
    live = old[22:23]
    state = jnp.where(live > 0.5, jnp.concatenate([x1, v1, a1, j1], axis=0), 0.0)
    state_ref[...] = state
    hot = one_hot(old[23:24].astype(jnp.int32), stars)
    rows = jnp.concatenate([state, jnp.broadcast_to(live, (4, slots))], axis=0)
    moved = exact_product(rows, hot, 1)
    active = moved[12:13] > 0.5
    new_pv_ref[...] = jnp.where(active, moved[0:6], pv_ref[...])
    new_aj_ref[...] = jnp.where(active, moved[6:12], aj_ref[...])


VMEM = pl.BlockSpec(memory_space=pltpu.VMEM)
HBM = pl.BlockSpec(memory_space=pltpu.HBM)


def cost(sources, slots):
    pairs = sum(s.size // 8 for s in sources) * slots
    return pl.CostEstimate(flops=pairs, bytes_accessed=4 * pairs // slots, transcendentals=pairs)


def call_pairs(sources, factors, acc):
    slots = factors.shape[1] // 2
    operands = list(sources) + [factors] + ([] if acc is None else [acc])
    return pl.pallas_call(
        functools.partial(pair_kernel, len(sources), acc is None),
        out_shape=jax.ShapeDtypeStruct((24, slots), f32),
        in_specs=[VMEM] * len(operands),
        out_specs=VMEM,
        scratch_shapes=[pltpu.VMEM((24, slots), f32)] + pair_scratch(sources, slots),
        compiler_params=PARAMS,
        cost_estimate=cost(sources, slots),
        name="pairs",
    )(*operands)


def per_device(n, slots, pos_vel, acc_jerk, star_mass, step_phase, step_level, counts, star_order):
    stars = pos_vel.shape[1]
    inputs = [pos_vel, acc_jerk] + [values.reshape(1, -1) for values in (star_mass, step_phase, step_level, counts)]
    inputs.append(star_order)
    own, old, factors = pl.pallas_call(
        functools.partial(prepare_kernel, slots),
        out_shape=(
            jax.ShapeDtypeStruct((8, stars), f32),
            jax.ShapeDtypeStruct((24, slots), f32),
            jax.ShapeDtypeStruct((FACTOR_ROWS, 2 * slots), bf16),
        ),
        in_specs=[HBM] * 7,
        out_specs=(VMEM,) * 3,
        scratch_shapes=[pltpu.VMEM(values.shape, values.dtype) for values in inputs] + [pltpu.SemaphoreType.DMA((7,))],
        compiler_params=PARAMS,
        name="prepare",
    )(*[pltpu.with_memory_space_constraint(values, pltpu.HBM) if values.size > 1 else values for values in inputs])

    def swap(values, bit):
        return lax.ppermute(values, "ja", [(i, i ^ bit) for i in range(n)])

    def after(acc, *values):
        return lax.optimization_barrier(values + (acc,))

    def pairs(acc, *sources):
        return call_pairs(sources, factors, acc)

    across = swap(own, 1)
    held, arrived, bit = own, own, n // 2
    coming = swap(own, bit)
    acc = pairs(None, own)
    acc = pairs(acc, across)
    while bit > 4:
        arrived, acc = after(acc, coming)
        held = jnp.concatenate([held, arrived], axis=0)
        bit //= 2
        across = swap(arrived, 1)
        beside = swap(held, 2) if bit == 4 else None
        coming = swap(held, bit)
        acc = pairs(acc, arrived)
        acc = pairs(acc, across)
    arrived, beside, acc = after(acc, coming, beside)
    beside_across = swap(beside, 1)
    across = swap(arrived, 1)
    coming = swap(arrived, 2)
    acc = pairs(acc, arrived, beside)
    acc = pairs(acc, across, beside_across)
    last, acc = after(acc, coming)
    across = swap(last, 1)
    acc = pairs(acc, last)
    return pl.pallas_call(
        functools.partial(finish_kernel, 1),
        out_shape=(
            jax.ShapeDtypeStruct(pos_vel.shape, f32),
            jax.ShapeDtypeStruct(acc_jerk.shape, f32),
            jax.ShapeDtypeStruct((12, slots), f32),
        ),
        in_specs=[VMEM] * 6,
        out_specs=(VMEM,) * 3,
        scratch_shapes=[pltpu.VMEM((24, slots), f32)] + pair_scratch([across], slots),
        compiler_params=PARAMS,
        cost_estimate=cost([across], slots),
        name="finish",
    )(across, factors, acc, old, pos_vel, acc_jerk)


A_DEV = 128


def solution(mesh):
    in_specs = (
        P(None, ("runs", "ja")),
        P(None, ("runs", "ja")),
        P(("runs", "ja")),
        P(("runs", "ja")),
        P(("runs", "ja")),
        P(("runs", "ja")),
        P(("runs", "ja"), None),
    )
    out_specs = (P(None, ("runs", "ja")), P(None, ("runs", "ja")), P(None, ("runs", "ja")))
    return jax.shard_map(
        functools.partial(per_device, mesh.shape["ja"], 2 * A_DEV),
        mesh=mesh,
        in_specs=in_specs,
        out_specs=out_specs,
        check_vma=False,
    )
```

```python
import functools

import jax
import jax.numpy as jnp
from jax import lax
from jax.experimental import pallas as pl
from jax.experimental.pallas import tpu as pltpu
from jax.sharding import PartitionSpec as P

soft_sq = 0.01
base_step = 2.0
f32 = jnp.float32
bf16 = jnp.bfloat16

CHUNK = 128
TOGETHER = 4
FACTOR_ROWS = 128
RING = 16
PARAMS = pltpu.CompilerParams(vmem_limit_bytes=32 << 20)


def round_bf16(values):
    return values.astype(bf16).astype(f32)


def split(values, terms):
    out = []
    for _ in range(terms - 1):
        head = round_bf16(values)
        out.append(head)
        values = values - head
    return out + [round_bf16(values)]


def four_terms(state):
    grid = jnp.floor(state * 4.0 + 0.5) * 0.25
    low = state - grid
    low1, low2, low3 = split(low, 3)
    return grid, low1, low2, low3, low


def row_index(state):
    return lax.broadcasted_iota(jnp.int32, state.shape, 0)


def down3(state):
    return jnp.concatenate([state[5:8], state[0:5]], axis=0)


def source_factors(state):
    row = row_index(state)
    grid, low1, low2, low3, low = four_terms(state)
    square = jnp.where(row == 6, 1.0, grid * grid)
    rest = jnp.where(row < 3, (2.0 * grid + low) * low, (grid + low) * down3(grid + low))
    rest1, rest2, rest3 = [jnp.where(row == 6, 1.0, term) for term in split(rest, 3)]
    square1 = round_bf16(square)
    square2 = jnp.where(row == 6, 1.0, square - square1)
    groups = [grid, square1, square2, grid, grid, grid, low1, low1, low1, low2, low2, low3, rest1, rest2, rest3]
    pad = [jnp.zeros_like(state)] * (FACTOR_ROWS // 8 - len(groups))
    return jnp.concatenate(groups + pad, axis=0).astype(bf16)


def target_factors(state):
    grid, low1, low2, low3, low = four_terms(state)
    zero, one = jnp.zeros_like(state), jnp.ones_like(state)
    z1, z2, z3 = zero[0:1], zero[0:2], zero[0:3]

    def add3(values):
        return values[0:1] + values[1:2] + values[2:3]

    def near(values):
        return jnp.concatenate([-2.0 * values[0:3], z3, z2], axis=0)

    def crossed(values):
        return jnp.concatenate([-values[3:6], -values[0:3], z2], axis=0)

    def sums(first, second, scalar):
        return jnp.concatenate([first, second, scalar, z1], axis=0)

    square1, square2 = split(add3(grid[0:3] * grid[0:3]), 2)
    rest = split(add3((2.0 * grid[0:3] + low[0:3]) * low[0:3]) + soft_sq, 3)
    moved = split(add3((grid + low)[0:3] * (grid + low)[3:6]), 3)
    o3 = one[0:3]
    dist = [near(grid), sums(o3, z3, square1), sums(o3, z3, square2), near(low1), near(low2), near(low3)]
    dist += [near(grid), near(low1), near(low2), near(grid), near(low1), near(grid)]
    dist += [sums(o3, z3, term) for term in rest]
    radial = [crossed(grid), zero, zero, crossed(low1), crossed(low2), crossed(low3)]
    radial += [crossed(grid), crossed(low1), crossed(low2), crossed(grid), crossed(low1), crossed(grid)]
    radial += [sums(z3, o3, term) for term in moved]
    pad = [zero] * (FACTOR_ROWS // 8 - len(dist))
    return jnp.concatenate(
        [jnp.concatenate(radial + pad, axis=0), jnp.concatenate(dist + pad, axis=0)], axis=1
    ).astype(bf16)


def sum_factors(state):
    row = row_index(state)
    mass = jnp.broadcast_to(state[6:7], state.shape)
    by_weight = mass * jnp.where(row < 6, state, jnp.where(row == 6, 1.0, 0.0))
    by_radial = mass * jnp.where(row < 3, 0.0, jnp.where(row < 6, -3.0 * down3(state), jnp.where(row == 7, 3.0, 0.0)))
    return (
        jnp.concatenate(split(by_weight, 3), axis=0).astype(bf16),
        jnp.concatenate(split(by_radial, 3), axis=0).astype(bf16),
    )


def add_pairs(states, factors, sums, scratch):
    slots = factors[0].shape[1] // 2
    products, weights = scratch[:RING], scratch[RING:]
    per, sets = states[0].shape[1] // CHUNK, len(factors)
    ready = {}

    def prepare(b):
        ready[b] = (source_factors(states[b]).T,) + sum_factors(states[b])

    def place(c):
        c = c // sets
        return c // per, slice(c % per * CHUNK, (c % per + 1) * CHUNK)

    def multiply(c):
        b, span = place(c)
        products[c % RING][...] = jnp.dot(ready[b][0][span], factors[c % sets], preferred_element_type=f32)

    def weigh(c):
        product, out = products[c % RING], weights[c % RING]
        for g in range(0, CHUNK, 16):
            for lane in range(0, slots, 128):
                cols = slice(lane, lane + 128)
                radial = product[g : g + 16, cols]
                dist_sq = product[g : g + 16, slots + lane : slots + lane + 128]
                inverse = lax.rsqrt(dist_sq)
                inverse_sq = inverse * inverse
                weight = inverse * inverse_sq
                radial = weight * (inverse_sq * radial)
                weight_hi, radial_hi = weight.astype(bf16), radial.astype(bf16)
                out[g : g + 16, cols] = weight_hi
                out[CHUNK + g : CHUNK + g + 16, cols] = (weight - weight_hi.astype(f32)).astype(bf16)
                out[2 * CHUNK + g : 2 * CHUNK + g + 16, cols] = radial_hi
                out[3 * CHUNK + g : 3 * CHUNK + g + 16, cols] = (radial - radial_hi.astype(f32)).astype(bf16)

    def total(c):
        b, span = place(c)
        left = [ready[b][1][:, span]] * 2 + [ready[b][2][:, span]] * 2
        sums[c % sets][...] += jnp.dot(
            jnp.concatenate(left, axis=1), weights[c % RING][...], preferred_element_type=f32
        )

    steps = len(states) * per * sets
    prepare(0)
    multiply(0)
    for c in range(steps):
        if (c + 2) % (per * sets) == 0 and (c + 2) // (per * sets) < len(states):
            prepare((c + 2) // (per * sets))
        if c + 1 < steps:
            multiply(c + 1)
        weigh(c)
        if c > 0:
            total(c - 1)
    total(steps - 1)


def add_blocks(sources, factors, sums, scratch):
    counts = [ref.shape[0] // 8 for ref in sources]
    if sum(counts) <= TOGETHER:
        rows = [ref[b : b + 8] for ref in sources for b in range(0, ref.shape[0], 8)]
        add_pairs(rows, factors, sums, scratch)
        return
    together = next(t for t in range(TOGETHER, 0, -1) if all(c % t == 0 for c in counts))
    for ref, count in zip(sources, counts):

        def step(i, _):
            rows = [ref[pl.ds(pl.multiple_of((i * together + b) * 8, 8), 8), :] for b in range(together)]
            add_pairs(rows, factors, sums, scratch)
            return 0

        lax.fori_loop(0, count // together, step, 0)


def pair_scratch(slots):
    return [pltpu.VMEM((CHUNK, 2 * slots), f32)] * RING + [pltpu.VMEM((4 * CHUNK, slots), bf16)] * RING


def one_hot(order, stars):
    row = lax.broadcasted_iota(jnp.int32, (stars, order.shape[1]), 0)
    return jnp.where(row == order, 1.0, 0.0).astype(f32).astype(bf16)


def spread(hot, live):
    rows = jnp.broadcast_to(live, (16, live.shape[1])).astype(bf16)
    return lax.dot_general(rows, hot, (((1,), (1,)), ((), ())), preferred_element_type=f32)[0:1]


def exact_product(rows, hot, contract):
    height = rows.shape[0]
    terms = jnp.concatenate(split(rows, 3), axis=0).astype(bf16)
    out = lax.dot_general(terms, hot, (((1,), (contract,)), ((), ())), preferred_element_type=f32)
    return out[0:height] + out[height : 2 * height] + out[2 * height : 3 * height]


def prepare_kernel(slots, *refs):
    inputs, (src_ref, tgt_ref, old_ref, fac_ref), here, sems = refs[:7], refs[7:11], refs[11:18], refs[18]
    copies = [pltpu.make_async_copy(src, dst, sems.at[i]) for i, (src, dst) in enumerate(zip(inputs, here))]
    for copy in copies:
        copy.start()
    pv_ref, aj_ref, mass_ref, phase_ref, level_ref, count_ref, order_ref = here
    stars = pv_ref.shape[1]
    copies[5].wait()
    copies[6].wait()
    order = order_ref[0:1, 0:slots]
    hot = one_hot(order, stars)
    live = jnp.where(lax.broadcasted_iota(jnp.int32, (1, slots), 1) < count_ref[...], 1.0, 0.0)
    active = spread(hot, live)
    for copy in copies[:5]:
        copy.wait()
    level = level_ref[...]
    step_len = base_step * jnp.where((level & 1) > 0, 0.5, 1.0) * jnp.where((level & 2) > 0, 0.25, 1.0)
    age = step_len * jnp.where(active > 0.5, 1.0, phase_ref[...])
    half_sq = 0.5 * age * age
    sixth_cube = age * age * age / 6.0
    pv, aj = pv_ref[...], aj_ref[...]
    x, v, a, j = pv[0:3], pv[3:6], aj[0:3], aj[3:6]
    position = x + age * v + half_sq * a + sixth_cube * j
    velocity = v + age * a + half_sq * j
    state = jnp.concatenate([position, velocity, mass_ref[...], step_len], axis=0)
    src_ref[...] = state
    gap = jnp.zeros((2, stars), f32)
    old = exact_product(jnp.concatenate([state, pv, gap, aj, gap], axis=0), hot, 0)
    tgt_ref[...] = old[0:8]
    old_ref[...] = jnp.concatenate([old[0:22], live, order.astype(f32)], axis=0)
    fac_ref[...] = target_factors(old[0:8])


def first_kernel(src_ref, mine_ref, theirs_ref, out_mine, out_theirs, fac_ref, *scratch):
    factors = target_factors(theirs_ref[...])
    fac_ref[...] = factors
    for out in (out_mine, out_theirs):
        out[...] = jnp.zeros_like(out)
    add_blocks([src_ref], [mine_ref[...], factors], [out_mine, out_theirs], scratch)


def pair_kernel(parts, sets, folded, *refs):
    sources, refs = refs[:parts], refs[parts:]
    factors, sums_in, outs, scratch = refs[:sets], refs[sets : 2 * sets], refs[2 * sets : 3 * sets], refs[3 * sets :]
    if folded:
        outs, folded_outs, scratch = scratch[:sets], outs, scratch[sets:]
    for out, sums in zip(outs, sums_in):
        out[...] = sums[...]
    add_blocks(sources, [ref[...] for ref in factors], outs, scratch)
    if folded:
        for out, sums in zip(folded_outs, outs):
            out[...] = sums[0:8] + sums[8:16] + sums[16:24]


def finish_kernel(mine_ref, other_ref, old_ref, pv_ref, aj_ref, new_pv_ref, new_aj_ref, state_ref):
    stars = pv_ref.shape[1]
    sums = mine_ref[...] + other_ref[...]
    old = old_ref[...]
    here, there, step_len = old[0:3], old[3:6], old[7:8]
    a1 = sums[0:3] - here * sums[6:7]
    j1 = sums[3:6] - there * sums[6:7] + here * sums[7:8]
    x0, v0, a0, j0 = old[8:11], old[11:14], old[16:19], old[19:22]
    half_step = 0.5 * step_len
    twelfth = step_len * step_len / 12.0
    v1 = v0 + half_step * (a0 + a1) + twelfth * (j0 - j1)
    x1 = x0 + half_step * (v0 + v1) + twelfth * (a0 - a1)
    live = old[22:23]
    state = jnp.where(live > 0.5, jnp.concatenate([x1, v1, a1, j1], axis=0), 0.0)
    state_ref[...] = state
    hot = one_hot(old[23:24].astype(jnp.int32), stars)
    rows = jnp.concatenate([state, jnp.broadcast_to(live, (4, live.shape[1]))], axis=0)
    moved = exact_product(rows, hot, 1)
    active = moved[12:13] > 0.5
    new_pv_ref[...] = jnp.where(active, moved[0:6], pv_ref[...])
    new_aj_ref[...] = jnp.where(active, moved[6:12], aj_ref[...])


VMEM = pl.BlockSpec(memory_space=pltpu.VMEM)
HBM = pl.BlockSpec(memory_space=pltpu.HBM)


def cost(sources, slots):
    pairs = sum(s.size // 8 for s in sources) * slots
    return pl.CostEstimate(flops=pairs, bytes_accessed=4 * pairs // slots, transcendentals=pairs)


def call_pairs(sources, factors, sums, folded=False):
    sets, slots = len(factors), factors[0].shape[1] // 2
    operands = list(sources) + list(factors) + list(sums)
    shape = (24, slots)
    return pl.pallas_call(
        functools.partial(pair_kernel, len(sources), sets, folded),
        out_shape=(jax.ShapeDtypeStruct((8, slots) if folded else shape, f32),) * sets,
        in_specs=[VMEM] * len(operands),
        out_specs=(VMEM,) * sets,
        scratch_shapes=[pltpu.VMEM(shape, f32)] * (sets if folded else 0) + pair_scratch(slots),
        compiler_params=PARAMS,
        cost_estimate=cost(sources, sets * slots),
        name="pairs",
    )(*operands)


def per_device(n, slots, pos_vel, acc_jerk, star_mass, step_phase, step_level, counts, star_order):
    stars = pos_vel.shape[1]
    inputs = [pos_vel, acc_jerk] + [values.reshape(1, -1) for values in (star_mass, step_phase, step_level, counts)]
    inputs.append(star_order)
    factor_shape = jax.ShapeDtypeStruct((FACTOR_ROWS, 2 * slots), bf16)
    own, targets, old, mine = pl.pallas_call(
        functools.partial(prepare_kernel, slots),
        out_shape=(
            jax.ShapeDtypeStruct((8, stars), f32),
            jax.ShapeDtypeStruct((8, slots), f32),
            jax.ShapeDtypeStruct((24, slots), f32),
            factor_shape,
        ),
        in_specs=[HBM] * 7,
        out_specs=(VMEM,) * 4,
        scratch_shapes=[pltpu.VMEM(values.shape, values.dtype) for values in inputs] + [pltpu.SemaphoreType.DMA((7,))],
        compiler_params=PARAMS,
        name="prepare",
    )(*[pltpu.with_memory_space_constraint(values, pltpu.HBM) if values.size > 1 else values for values in inputs])

    def swap(values, bit):
        return lax.ppermute(values, "ja", [(i, i ^ bit) for i in range(n)])

    def after(sums, *values):
        *values, first, second = lax.optimization_barrier(values + tuple(sums))
        return *values, (first, second)

    theirs = swap(targets, 1)
    held, arrived, bit = own, own, n // 2
    coming = swap(own, bit)
    *sums, theirs = pl.pallas_call(
        first_kernel,
        out_shape=(jax.ShapeDtypeStruct((24, slots), f32),) * 2 + (factor_shape,),
        in_specs=[VMEM] * 3,
        out_specs=(VMEM,) * 3,
        scratch_shapes=pair_scratch(slots),
        compiler_params=PARAMS,
        cost_estimate=cost([own], 2 * slots),
        name="first",
    )(own, mine, theirs)
    both = (mine, theirs)
    while bit > 4:
        arrived, sums = after(sums, coming)
        held = jnp.concatenate([held, arrived], axis=0)
        bit //= 2
        beside = swap(held, 2) if bit == 4 else None
        coming = swap(held, bit)
        sums = call_pairs([arrived], both, sums)
    arrived, beside, sums = after(sums, coming, beside)
    coming = swap(arrived, 2)
    sums = call_pairs([arrived, beside], both, sums)
    last, sums = after(sums, coming)
    (for_them,) = call_pairs([last], [theirs], [sums[1]], folded=True)
    from_them = swap(for_them, 1)
    (here,) = call_pairs([last], [mine], [sums[0]], folded=True)
    return pl.pallas_call(
        finish_kernel,
        out_shape=(
            jax.ShapeDtypeStruct(pos_vel.shape, f32),
            jax.ShapeDtypeStruct(acc_jerk.shape, f32),
            jax.ShapeDtypeStruct((12, slots), f32),
        ),
        in_specs=[VMEM] * 5,
        out_specs=(VMEM,) * 3,
        compiler_params=PARAMS,
        name="finish",
    )(here, from_them, old, pos_vel, acc_jerk)


A_DEV = 128


def solution(mesh):
    in_specs = (
        P(None, ("runs", "ja")),
        P(None, ("runs", "ja")),
        P(("runs", "ja")),
        P(("runs", "ja")),
        P(("runs", "ja")),
        P(("runs", "ja")),
        P(("runs", "ja"), None),
    )
    out_specs = (P(None, ("runs", "ja")), P(None, ("runs", "ja")), P(None, ("runs", "ja")))
    return jax.shard_map(
        functools.partial(per_device, mesh.shape["ja"], 2 * A_DEV),
        mesh=mesh,
        in_specs=in_specs,
        out_specs=out_specs,
        check_vma=False,
    )
```

```python
import functools

import jax
import jax.numpy as jnp
from jax import lax
from jax.experimental import pallas as pl
from jax.experimental.pallas import tpu as pltpu
from jax.sharding import PartitionSpec as P

soft_sq = 0.01
base_step = 2.0
f32 = jnp.float32
bf16 = jnp.bfloat16

CHUNK = 128
TOGETHER = 4
FACTOR_ROWS = 128
PARAMS = pltpu.CompilerParams(vmem_limit_bytes=32 << 20)


def round_bf16(values):
    return values.astype(bf16).astype(f32)


def split(values, terms):
    out = []
    for _ in range(terms - 1):
        head = round_bf16(values)
        out.append(head)
        values = values - head
    return out + [round_bf16(values)]


def four_terms(state):
    grid = jnp.floor(state * 4.0 + 0.5) * 0.25
    low = state - grid
    low1, low2, low3 = split(low, 3)
    return grid, low1, low2, low3, low


def row_index(state):
    return lax.broadcasted_iota(jnp.int32, state.shape, 0)


def down3(state):
    return jnp.concatenate([state[5:8], state[0:5]], axis=0)


def source_factors(state):
    row = row_index(state)
    grid, low1, low2, low3, low = four_terms(state)
    square = jnp.where(row == 6, 1.0, grid * grid)
    rest = jnp.where(row < 3, (2.0 * grid + low) * low, (grid + low) * down3(grid + low))
    rest1, rest2, rest3 = [jnp.where(row == 6, 1.0, term) for term in split(rest, 3)]
    square1 = round_bf16(square)
    square2 = jnp.where(row == 6, 1.0, square - square1)
    groups = [grid, square1, square2, grid, grid, grid, low1, low1, low1, low2, low2, low3, rest1, rest2, rest3]
    pad = [jnp.zeros_like(state)] * (FACTOR_ROWS // 8 - len(groups))
    return jnp.concatenate(groups + pad, axis=0).astype(bf16)


def target_factors(state):
    grid, low1, low2, low3, low = four_terms(state)
    zero, one = jnp.zeros_like(state), jnp.ones_like(state)
    z1, z2, z3 = zero[0:1], zero[0:2], zero[0:3]

    def add3(values):
        return values[0:1] + values[1:2] + values[2:3]

    def near(values):
        return jnp.concatenate([-2.0 * values[0:3], z3, z2], axis=0)

    def crossed(values):
        return jnp.concatenate([-values[3:6], -values[0:3], z2], axis=0)

    def sums(first, second, scalar):
        return jnp.concatenate([first, second, scalar, z1], axis=0)

    square1, square2 = split(add3(grid[0:3] * grid[0:3]), 2)
    rest = split(add3((2.0 * grid[0:3] + low[0:3]) * low[0:3]) + soft_sq, 3)
    moved = split(add3((grid + low)[0:3] * (grid + low)[3:6]), 3)
    o3 = one[0:3]
    dist = [near(grid), sums(o3, z3, square1), sums(o3, z3, square2), near(low1), near(low2), near(low3)]
    dist += [near(grid), near(low1), near(low2), near(grid), near(low1), near(grid)]
    dist += [sums(o3, z3, term) for term in rest]
    radial = [crossed(grid), zero, zero, crossed(low1), crossed(low2), crossed(low3)]
    radial += [crossed(grid), crossed(low1), crossed(low2), crossed(grid), crossed(low1), crossed(grid)]
    radial += [sums(z3, o3, term) for term in moved]
    pad = [zero] * (FACTOR_ROWS // 8 - len(dist))
    return jnp.concatenate(
        [jnp.concatenate(radial + pad, axis=0), jnp.concatenate(dist + pad, axis=0)], axis=1
    ).astype(bf16)


def sum_factors(state):
    row = row_index(state)
    mass = jnp.broadcast_to(state[6:7], state.shape)
    by_weight = mass * jnp.where(row < 6, state, jnp.where(row == 6, 1.0, 0.0))
    by_radial = mass * jnp.where(row < 3, 0.0, jnp.where(row < 6, -3.0 * down3(state), jnp.where(row == 7, 3.0, 0.0)))
    return (
        jnp.concatenate(split(by_weight, 3), axis=0).astype(bf16),
        jnp.concatenate(split(by_radial, 3), axis=0).astype(bf16),
    )


def pair_weights(products):
    sources, slots = products.shape[0], products.shape[1] // 2
    parts = [[], [], [], []]
    for g in range(0, sources, 16):
        rows = [[], [], [], []]
        for lane in range(0, slots, 128):
            radial = products[g : g + 16, lane : lane + 128]
            dist_sq = products[g : g + 16, slots + lane : slots + lane + 128]
            inverse = lax.rsqrt(dist_sq)
            inverse_sq = inverse * inverse
            weight = inverse * inverse_sq
            radial = weight * (inverse_sq * radial)
            weight_hi, radial_hi = weight.astype(bf16), radial.astype(bf16)
            rows[0].append(weight_hi)
            rows[1].append((weight - weight_hi.astype(f32)).astype(bf16))
            rows[2].append(radial_hi)
            rows[3].append((radial - radial_hi.astype(f32)).astype(bf16))
        for part, row in zip(parts, rows):
            part.append(jnp.concatenate(row, axis=1))
    return jnp.concatenate(parts[0] + parts[1] + parts[2] + parts[3], axis=0)


def add_pairs(states, factors, sums):
    for state in states:
        factors_s = source_factors(state).T
        by_weight, by_radial = sum_factors(state)
        for at in range(0, state.shape[1], CHUNK):
            span = slice(at, at + CHUNK)
            left = jnp.concatenate([by_weight[:, span]] * 2 + [by_radial[:, span]] * 2, axis=1)
            for factors_t, out in zip(factors, sums):
                products = jnp.dot(factors_s[span], factors_t, preferred_element_type=f32)
                out[...] += jnp.dot(left, pair_weights(products), preferred_element_type=f32)


def add_blocks(sources, factors, sums):
    counts = [ref.shape[0] // 8 for ref in sources]
    if sum(counts) <= TOGETHER:
        rows = [ref[b : b + 8] for ref in sources for b in range(0, ref.shape[0], 8)]
        add_pairs(rows, factors, sums)
        return
    together = next(t for t in range(TOGETHER, 0, -1) if all(c % t == 0 for c in counts))
    for ref, count in zip(sources, counts):

        def step(i, _):
            rows = [ref[pl.ds(pl.multiple_of((i * together + b) * 8, 8), 8), :] for b in range(together)]
            add_pairs(rows, factors, sums)
            return 0

        lax.fori_loop(0, count // together, step, 0)


def one_hot(order, stars):
    row = lax.broadcasted_iota(jnp.int32, (stars, order.shape[1]), 0)
    return jnp.where(row == order, 1.0, 0.0).astype(f32).astype(bf16)


def spread(hot, live):
    rows = jnp.broadcast_to(live, (16, live.shape[1])).astype(bf16)
    return lax.dot_general(rows, hot, (((1,), (1,)), ((), ())), preferred_element_type=f32)[0:1]


def exact_product(rows, hot, contract):
    height = rows.shape[0]
    terms = jnp.concatenate(split(rows, 3), axis=0).astype(bf16)
    out = lax.dot_general(terms, hot, (((1,), (contract,)), ((), ())), preferred_element_type=f32)
    return out[0:height] + out[height : 2 * height] + out[2 * height : 3 * height]


def prepare_kernel(slots, *refs):
    inputs, (src_ref, tgt_ref, old_ref, fac_ref), here, sems = refs[:7], refs[7:11], refs[11:18], refs[18]
    copies = [pltpu.make_async_copy(src, dst, sems.at[i]) for i, (src, dst) in enumerate(zip(inputs, here))]
    for copy in copies:
        copy.start()
    pv_ref, aj_ref, mass_ref, phase_ref, level_ref, count_ref, order_ref = here
    stars = pv_ref.shape[1]
    copies[5].wait()
    copies[6].wait()
    order = order_ref[0:1, 0:slots]
    hot = one_hot(order, stars)
    live = jnp.where(lax.broadcasted_iota(jnp.int32, (1, slots), 1) < count_ref[...], 1.0, 0.0)
    active = spread(hot, live)
    for copy in copies[:5]:
        copy.wait()
    level = level_ref[...]
    step_len = base_step * jnp.where((level & 1) > 0, 0.5, 1.0) * jnp.where((level & 2) > 0, 0.25, 1.0)
    age = step_len * jnp.where(active > 0.5, 1.0, phase_ref[...])
    half_sq = 0.5 * age * age
    sixth_cube = age * age * age / 6.0
    pv, aj = pv_ref[...], aj_ref[...]
    x, v, a, j = pv[0:3], pv[3:6], aj[0:3], aj[3:6]
    position = x + age * v + half_sq * a + sixth_cube * j
    velocity = v + age * a + half_sq * j
    state = jnp.concatenate([position, velocity, mass_ref[...], step_len], axis=0)
    src_ref[...] = state
    gap = jnp.zeros((2, stars), f32)
    old = exact_product(jnp.concatenate([state, pv, gap, aj, gap], axis=0), hot, 0)
    tgt_ref[...] = old[0:8]
    old_ref[...] = jnp.concatenate([old[0:22], live, order.astype(f32)], axis=0)
    fac_ref[...] = target_factors(old[0:8])


def first_kernel(src_ref, mine_ref, theirs_ref, out_mine, out_theirs, fac_ref):
    factors = target_factors(theirs_ref[...])
    fac_ref[...] = factors
    for out in (out_mine, out_theirs):
        out[...] = jnp.zeros_like(out)
    add_blocks([src_ref], [mine_ref[...], factors], [out_mine, out_theirs])


def pair_kernel(parts, sets, folded, *refs):
    sources, refs = refs[:parts], refs[parts:]
    factors, sums_in, outs, rest = refs[:sets], refs[sets : 2 * sets], refs[2 * sets : 3 * sets], refs[3 * sets :]
    if folded:
        outs, folded_outs = rest, outs
    for out, sums in zip(outs, sums_in):
        out[...] = sums[...]
    add_blocks(sources, [ref[...] for ref in factors], outs)
    if folded:
        for out, sums in zip(folded_outs, outs):
            out[...] = sums[0:8] + sums[8:16] + sums[16:24]


def finish_kernel(mine_ref, other_ref, old_ref, pv_ref, aj_ref, new_pv_ref, new_aj_ref, state_ref):
    stars = pv_ref.shape[1]
    sums = mine_ref[...] + other_ref[...]
    old = old_ref[...]
    here, there, step_len = old[0:3], old[3:6], old[7:8]
    a1 = sums[0:3] - here * sums[6:7]
    j1 = sums[3:6] - there * sums[6:7] + here * sums[7:8]
    x0, v0, a0, j0 = old[8:11], old[11:14], old[16:19], old[19:22]
    half_step = 0.5 * step_len
    twelfth = step_len * step_len / 12.0
    v1 = v0 + half_step * (a0 + a1) + twelfth * (j0 - j1)
    x1 = x0 + half_step * (v0 + v1) + twelfth * (a0 - a1)
    live = old[22:23]
    state = jnp.where(live > 0.5, jnp.concatenate([x1, v1, a1, j1], axis=0), 0.0)
    state_ref[...] = state
    hot = one_hot(old[23:24].astype(jnp.int32), stars)
    rows = jnp.concatenate([state, jnp.broadcast_to(live, (4, live.shape[1]))], axis=0)
    moved = exact_product(rows, hot, 1)
    active = moved[12:13] > 0.5
    new_pv_ref[...] = jnp.where(active, moved[0:6], pv_ref[...])
    new_aj_ref[...] = jnp.where(active, moved[6:12], aj_ref[...])


VMEM = pl.BlockSpec(memory_space=pltpu.VMEM)
HBM = pl.BlockSpec(memory_space=pltpu.HBM)


def cost(sources, slots):
    pairs = sum(s.size // 8 for s in sources) * slots
    return pl.CostEstimate(flops=pairs, bytes_accessed=4 * pairs // slots, transcendentals=pairs)


def call_pairs(sources, factors, sums, folded=False):
    sets, slots = len(factors), factors[0].shape[1] // 2
    operands = list(sources) + list(factors) + list(sums)
    shape = (24, slots)
    return pl.pallas_call(
        functools.partial(pair_kernel, len(sources), sets, folded),
        out_shape=(jax.ShapeDtypeStruct((8, slots) if folded else shape, f32),) * sets,
        in_specs=[VMEM] * len(operands),
        out_specs=(VMEM,) * sets,
        scratch_shapes=[pltpu.VMEM(shape, f32)] * (sets if folded else 0),
        compiler_params=PARAMS,
        cost_estimate=cost(sources, sets * slots),
        name="pairs",
    )(*operands)


def per_device(n, slots, pos_vel, acc_jerk, star_mass, step_phase, step_level, counts, star_order):
    stars = pos_vel.shape[1]
    inputs = [pos_vel, acc_jerk] + [values.reshape(1, -1) for values in (star_mass, step_phase, step_level, counts)]
    inputs.append(star_order)
    factor_shape = jax.ShapeDtypeStruct((FACTOR_ROWS, 2 * slots), bf16)
    own, targets, old, mine = pl.pallas_call(
        functools.partial(prepare_kernel, slots),
        out_shape=(
            jax.ShapeDtypeStruct((8, stars), f32),
            jax.ShapeDtypeStruct((8, slots), f32),
            jax.ShapeDtypeStruct((24, slots), f32),
            factor_shape,
        ),
        in_specs=[HBM] * 7,
        out_specs=(VMEM,) * 4,
        scratch_shapes=[pltpu.VMEM(values.shape, values.dtype) for values in inputs] + [pltpu.SemaphoreType.DMA((7,))],
        compiler_params=PARAMS,
        name="prepare",
    )(*[pltpu.with_memory_space_constraint(values, pltpu.HBM) if values.size > 1 else values for values in inputs])

    def swap(values, bit):
        return lax.ppermute(values, "ja", [(i, i ^ bit) for i in range(n)])

    def after(sums, *values):
        *values, first, second = lax.optimization_barrier(values + tuple(sums))
        return *values, (first, second)

    theirs = swap(targets, 1)
    held, arrived, bit = own, own, n // 2
    coming = swap(own, bit)
    *sums, theirs = pl.pallas_call(
        first_kernel,
        out_shape=(jax.ShapeDtypeStruct((24, slots), f32),) * 2 + (factor_shape,),
        in_specs=[VMEM] * 3,
        out_specs=(VMEM,) * 3,
        compiler_params=PARAMS,
        cost_estimate=cost([own], 2 * slots),
        name="first",
    )(own, mine, theirs)
    both = (mine, theirs)
    while bit > 4:
        arrived, sums = after(sums, coming)
        held = jnp.concatenate([held, arrived], axis=0)
        bit //= 2
        beside = swap(held, 2) if bit == 4 else None
        coming = swap(held, bit)
        sums = call_pairs([arrived], both, sums)
    arrived, sums = after(sums, coming)
    coming = swap(arrived, 2)
    beside, sums = after(sums, beside)
    sums = call_pairs([arrived, beside], both, sums)
    last, sums = after(sums, coming)
    (for_them,) = call_pairs([last], [theirs], [sums[1]], folded=True)
    from_them = swap(for_them, 1)
    (here,) = call_pairs([last], [mine], [sums[0]], folded=True)
    return pl.pallas_call(
        finish_kernel,
        out_shape=(
            jax.ShapeDtypeStruct(pos_vel.shape, f32),
            jax.ShapeDtypeStruct(acc_jerk.shape, f32),
            jax.ShapeDtypeStruct((12, slots), f32),
        ),
        in_specs=[VMEM] * 5,
        out_specs=(VMEM,) * 3,
        compiler_params=PARAMS,
        name="finish",
    )(here, from_them, old, pos_vel, acc_jerk)


A_DEV = 128


def solution(mesh):
    in_specs = (
        P(None, ("runs", "ja")),
        P(None, ("runs", "ja")),
        P(("runs", "ja")),
        P(("runs", "ja")),
        P(("runs", "ja")),
        P(("runs", "ja")),
        P(("runs", "ja"), None),
    )
    out_specs = (P(None, ("runs", "ja")), P(None, ("runs", "ja")), P(None, ("runs", "ja")))
    return jax.shard_map(
        functools.partial(per_device, mesh.shape["ja"], 2 * A_DEV),
        mesh=mesh,
        in_specs=in_specs,
        out_specs=out_specs,
        check_vma=False,
    )
```

```python
import functools

import jax
import jax.numpy as jnp
from jax import lax
from jax.experimental import pallas as pl
from jax.experimental.pallas import tpu as pltpu
from jax.sharding import PartitionSpec as P

soft_sq = 0.01
base_step = 2.0
f32 = jnp.float32
bf16 = jnp.bfloat16

CHUNK = 128
TOGETHER = 4
FACTOR_ROWS = 128
PARAMS = pltpu.CompilerParams(vmem_limit_bytes=32 << 20)


def round_bf16(values):
    return values.astype(bf16).astype(f32)


def split(values, terms):
    out = []
    for _ in range(terms - 1):
        head = round_bf16(values)
        out.append(head)
        values = values - head
    return out + [round_bf16(values)]


def four_terms(state):
    grid = jnp.floor(state * 4.0 + 0.5) * 0.25
    low = state - grid
    low1, low2, low3 = split(low, 3)
    return grid, low1, low2, low3, low


def row_index(state):
    return lax.broadcasted_iota(jnp.int32, state.shape, 0)


def down3(state):
    return jnp.concatenate([state[5:8], state[0:5]], axis=0)


def source_factors(state):
    row = row_index(state)
    grid, low1, low2, low3, low = four_terms(state)
    square = jnp.where(row == 6, 1.0, grid * grid)
    rest = jnp.where(row < 3, (2.0 * grid + low) * low, (grid + low) * down3(grid + low))
    rest1, rest2, rest3 = [jnp.where(row == 6, 1.0, term) for term in split(rest, 3)]
    square1 = round_bf16(square)
    square2 = jnp.where(row == 6, 1.0, square - square1)
    groups = [grid, square1, square2, grid, grid, grid, low1, low1, low1, low2, low2, low3, rest1, rest2, rest3]
    pad = [jnp.zeros_like(state)] * (FACTOR_ROWS // 8 - len(groups))
    return jnp.concatenate(groups + pad, axis=0).astype(bf16)


def target_factors(state):
    grid, low1, low2, low3, low = four_terms(state)
    zero, one = jnp.zeros_like(state), jnp.ones_like(state)
    z1, z2, z3 = zero[0:1], zero[0:2], zero[0:3]

    def add3(values):
        return values[0:1] + values[1:2] + values[2:3]

    def near(values):
        return jnp.concatenate([-2.0 * values[0:3], z3, z2], axis=0)

    def crossed(values):
        return jnp.concatenate([-values[3:6], -values[0:3], z2], axis=0)

    def sums(first, second, scalar):
        return jnp.concatenate([first, second, scalar, z1], axis=0)

    square1, square2 = split(add3(grid[0:3] * grid[0:3]), 2)
    rest = split(add3((2.0 * grid[0:3] + low[0:3]) * low[0:3]) + soft_sq, 3)
    moved = split(add3((grid + low)[0:3] * (grid + low)[3:6]), 3)
    o3 = one[0:3]
    dist = [near(grid), sums(o3, z3, square1), sums(o3, z3, square2), near(low1), near(low2), near(low3)]
    dist += [near(grid), near(low1), near(low2), near(grid), near(low1), near(grid)]
    dist += [sums(o3, z3, term) for term in rest]
    radial = [crossed(grid), zero, zero, crossed(low1), crossed(low2), crossed(low3)]
    radial += [crossed(grid), crossed(low1), crossed(low2), crossed(grid), crossed(low1), crossed(grid)]
    radial += [sums(z3, o3, term) for term in moved]
    pad = [zero] * (FACTOR_ROWS // 8 - len(dist))
    return jnp.concatenate(
        [jnp.concatenate(radial + pad, axis=0), jnp.concatenate(dist + pad, axis=0)], axis=1
    ).astype(bf16)


def sum_factors(state):
    row = row_index(state)
    mass = jnp.broadcast_to(state[6:7], state.shape)
    by_weight = mass * jnp.where(row < 6, state, jnp.where(row == 6, 1.0, 0.0))
    by_radial = mass * jnp.where(row < 3, 0.0, jnp.where(row < 6, -3.0 * down3(state), jnp.where(row == 7, 3.0, 0.0)))
    return (
        jnp.concatenate(split(by_weight, 3), axis=0).astype(bf16),
        jnp.concatenate(split(by_radial, 3), axis=0).astype(bf16),
    )


def pair_weights(products):
    sources, slots = products.shape[0], products.shape[1] // 2
    parts = [[], [], [], []]
    for g in range(0, sources, 16):
        rows = [[], [], [], []]
        for lane in range(0, slots, 128):
            radial = products[g : g + 16, lane : lane + 128]
            dist_sq = products[g : g + 16, slots + lane : slots + lane + 128]
            inverse = lax.rsqrt(dist_sq)
            inverse_sq = inverse * inverse
            weight = inverse * inverse_sq
            radial = weight * (inverse_sq * radial)
            weight_hi, radial_hi = weight.astype(bf16), radial.astype(bf16)
            rows[0].append(weight_hi)
            rows[1].append((weight - weight_hi.astype(f32)).astype(bf16))
            rows[2].append(radial_hi)
            rows[3].append((radial - radial_hi.astype(f32)).astype(bf16))
        for part, row in zip(parts, rows):
            part.append(jnp.concatenate(row, axis=1))
    return jnp.concatenate(parts[0] + parts[1] + parts[2] + parts[3], axis=0)


def add_pairs(states, factors, sums):
    for state in states:
        factors_s = source_factors(state).T
        by_weight, by_radial = sum_factors(state)
        for at in range(0, state.shape[1], CHUNK):
            span = slice(at, at + CHUNK)
            left = jnp.concatenate([by_weight[:, span]] * 2 + [by_radial[:, span]] * 2, axis=1)
            for factors_t, out in zip(factors, sums):
                products = jnp.dot(factors_s[span], factors_t, preferred_element_type=f32)
                out[...] += jnp.dot(left, pair_weights(products), preferred_element_type=f32)


def add_blocks(sources, factors, sums):
    counts = [ref.shape[0] // 8 for ref in sources]
    if sum(counts) <= TOGETHER:
        rows = [ref[b : b + 8] for ref in sources for b in range(0, ref.shape[0], 8)]
        add_pairs(rows, factors, sums)
        return
    together = next(t for t in range(TOGETHER, 0, -1) if all(c % t == 0 for c in counts))
    for ref, count in zip(sources, counts):

        def step(i, _):
            rows = [ref[pl.ds(pl.multiple_of((i * together + b) * 8, 8), 8), :] for b in range(together)]
            add_pairs(rows, factors, sums)
            return 0

        lax.fori_loop(0, count // together, step, 0)


def one_hot(order, stars):
    row = lax.broadcasted_iota(jnp.int32, (stars, order.shape[1]), 0)
    return jnp.where(row == order, 1.0, 0.0).astype(f32).astype(bf16)


def spread(hot, live):
    rows = jnp.broadcast_to(live, (16, live.shape[1])).astype(bf16)
    return lax.dot_general(rows, hot, (((1,), (1,)), ((), ())), preferred_element_type=f32)[0:1]


def exact_product(rows, hot, contract):
    height = rows.shape[0]
    terms = jnp.concatenate(split(rows, 3), axis=0).astype(bf16)
    out = lax.dot_general(terms, hot, (((1,), (contract,)), ((), ())), preferred_element_type=f32)
    return out[0:height] + out[height : 2 * height] + out[2 * height : 3 * height]


def prepare_kernel(slots, *refs):
    inputs, (src_ref, tgt_ref, old_ref, fac_ref), here, sems = refs[:7], refs[7:11], refs[11:18], refs[18]
    copies = [pltpu.make_async_copy(src, dst, sems.at[i]) for i, (src, dst) in enumerate(zip(inputs, here))]
    for copy in copies:
        copy.start()
    pv_ref, aj_ref, mass_ref, phase_ref, level_ref, count_ref, order_ref = here
    stars = pv_ref.shape[1]
    copies[5].wait()
    copies[6].wait()
    order = order_ref[0:1, 0:slots]
    hot = one_hot(order, stars)
    live = jnp.where(lax.broadcasted_iota(jnp.int32, (1, slots), 1) < count_ref[...], 1.0, 0.0)
    active = spread(hot, live)
    for copy in copies[:5]:
        copy.wait()
    level = level_ref[...]
    step_len = base_step * jnp.where((level & 1) > 0, 0.5, 1.0) * jnp.where((level & 2) > 0, 0.25, 1.0)
    age = step_len * jnp.where(active > 0.5, 1.0, phase_ref[...])
    half_sq = 0.5 * age * age
    sixth_cube = age * age * age / 6.0
    pv, aj = pv_ref[...], aj_ref[...]
    x, v, a, j = pv[0:3], pv[3:6], aj[0:3], aj[3:6]
    position = x + age * v + half_sq * a + sixth_cube * j
    velocity = v + age * a + half_sq * j
    state = jnp.concatenate([position, velocity, mass_ref[...], step_len], axis=0)
    src_ref[...] = state
    gap = jnp.zeros((2, stars), f32)
    old = exact_product(jnp.concatenate([state, pv, gap, aj, gap], axis=0), hot, 0)
    tgt_ref[...] = old[0:8]
    old_ref[...] = jnp.concatenate([old[0:22], live, order.astype(f32)], axis=0)
    fac_ref[...] = target_factors(old[0:8])


def first_kernel(src_ref, mine_ref, theirs_ref, out_mine, out_theirs, fac_ref):
    factors = target_factors(theirs_ref[...])
    fac_ref[...] = factors
    for out in (out_mine, out_theirs):
        out[...] = jnp.zeros_like(out)
    add_blocks([src_ref], [mine_ref[...], factors], [out_mine, out_theirs])


def pair_kernel(parts, sets, folded, *refs):
    sources, refs = refs[:parts], refs[parts:]
    factors, sums_in, outs, rest = refs[:sets], refs[sets : 2 * sets], refs[2 * sets : 3 * sets], refs[3 * sets :]
    if folded:
        outs, folded_outs = rest, outs
    for out, sums in zip(outs, sums_in):
        out[...] = sums[...]
    add_blocks(sources, [ref[...] for ref in factors], outs)
    if folded:
        for out, sums in zip(folded_outs, outs):
            out[...] = sums[0:8] + sums[8:16] + sums[16:24]


def finish_kernel(mine_ref, other_ref, old_ref, pv_ref, aj_ref, new_pv_ref, new_aj_ref, state_ref):
    stars = pv_ref.shape[1]
    sums = mine_ref[...] + other_ref[...]
    old = old_ref[...]
    here, there, step_len = old[0:3], old[3:6], old[7:8]
    a1 = sums[0:3] - here * sums[6:7]
    j1 = sums[3:6] - there * sums[6:7] + here * sums[7:8]
    x0, v0, a0, j0 = old[8:11], old[11:14], old[16:19], old[19:22]
    half_step = 0.5 * step_len
    twelfth = step_len * step_len / 12.0
    v1 = v0 + half_step * (a0 + a1) + twelfth * (j0 - j1)
    x1 = x0 + half_step * (v0 + v1) + twelfth * (a0 - a1)
    live = old[22:23]
    state = jnp.where(live > 0.5, jnp.concatenate([x1, v1, a1, j1], axis=0), 0.0)
    state_ref[...] = state
    hot = one_hot(old[23:24].astype(jnp.int32), stars)
    rows = jnp.concatenate([state, jnp.broadcast_to(live, (4, live.shape[1]))], axis=0)
    moved = exact_product(rows, hot, 1)
    active = moved[12:13] > 0.5
    new_pv_ref[...] = jnp.where(active, moved[0:6], pv_ref[...])
    new_aj_ref[...] = jnp.where(active, moved[6:12], aj_ref[...])


VMEM = pl.BlockSpec(memory_space=pltpu.VMEM)
HBM = pl.BlockSpec(memory_space=pltpu.HBM)


def cost(sources, slots):
    pairs = sum(s.size // 8 for s in sources) * slots
    return pl.CostEstimate(flops=pairs, bytes_accessed=4 * pairs // slots, transcendentals=pairs)


def call_pairs(sources, factors, sums, folded=False):
    sets, slots = len(factors), factors[0].shape[1] // 2
    operands = list(sources) + list(factors) + list(sums)
    shape = (24, slots)
    return pl.pallas_call(
        functools.partial(pair_kernel, len(sources), sets, folded),
        out_shape=(jax.ShapeDtypeStruct((8, slots) if folded else shape, f32),) * sets,
        in_specs=[VMEM] * len(operands),
        out_specs=(VMEM,) * sets,
        scratch_shapes=[pltpu.VMEM(shape, f32)] * (sets if folded else 0),
        compiler_params=PARAMS,
        cost_estimate=cost(sources, sets * slots),
        name="pairs",
    )(*operands)


def per_device(n, slots, pos_vel, acc_jerk, star_mass, step_phase, step_level, counts, star_order):
    stars = pos_vel.shape[1]
    inputs = [pos_vel, acc_jerk] + [values.reshape(1, -1) for values in (star_mass, step_phase, step_level, counts)]
    inputs.append(star_order)
    factor_shape = jax.ShapeDtypeStruct((FACTOR_ROWS, 2 * slots), bf16)
    own, targets, old, mine = pl.pallas_call(
        functools.partial(prepare_kernel, slots),
        out_shape=(
            jax.ShapeDtypeStruct((8, stars), f32),
            jax.ShapeDtypeStruct((8, slots), f32),
            jax.ShapeDtypeStruct((24, slots), f32),
            factor_shape,
        ),
        in_specs=[HBM] * 7,
        out_specs=(VMEM,) * 4,
        scratch_shapes=[pltpu.VMEM(values.shape, values.dtype) for values in inputs] + [pltpu.SemaphoreType.DMA((7,))],
        compiler_params=PARAMS,
        name="prepare",
    )(*[pltpu.with_memory_space_constraint(values, pltpu.HBM) if values.size > 1 else values for values in inputs])

    def swap(values, bit):
        return lax.ppermute(values, "ja", [(i, i ^ bit) for i in range(n)])

    def after(sums, *values):
        *values, first, second = lax.optimization_barrier(values + tuple(sums))
        return *values, (first, second)

    theirs = swap(targets, 1)
    held, bit = own, n // 2
    near = swap(held, 4) if bit == 8 else None
    coming = swap(held, bit)
    *sums, theirs = pl.pallas_call(
        first_kernel,
        out_shape=(jax.ShapeDtypeStruct((24, slots), f32),) * 2 + (factor_shape,),
        in_specs=[VMEM] * 3,
        out_specs=(VMEM,) * 3,
        compiler_params=PARAMS,
        cost_estimate=cost([own], 2 * slots),
        name="first",
    )(own, mine, theirs)
    both = (mine, theirs)
    while bit > 8:
        arrived, sums = after(sums, coming)
        held = jnp.concatenate([held, arrived], axis=0)
        bit //= 2
        near = swap(held, 4) if bit == 8 else None
        coming = swap(held, bit)
        sums = call_pairs([arrived], both, sums)
    arrived, sums = after(sums, coming)
    beside = swap(jnp.concatenate([held, arrived], axis=0), 2)
    coming = swap(arrived, 4)
    near, sums = after(sums, near)
    sums = call_pairs([arrived, near], both, sums)
    arrived, sums = after(sums, coming)
    coming = swap(jnp.concatenate([near, arrived], axis=0), 2)
    beside, sums = after(sums, beside)
    sums = call_pairs([arrived, beside], both, sums)
    last, sums = after(sums, coming)
    (for_them,) = call_pairs([last], [theirs], [sums[1]], folded=True)
    from_them = swap(for_them, 1)
    (here,) = call_pairs([last], [mine], [sums[0]], folded=True)
    return pl.pallas_call(
        finish_kernel,
        out_shape=(
            jax.ShapeDtypeStruct(pos_vel.shape, f32),
            jax.ShapeDtypeStruct(acc_jerk.shape, f32),
            jax.ShapeDtypeStruct((12, slots), f32),
        ),
        in_specs=[VMEM] * 5,
        out_specs=(VMEM,) * 3,
        compiler_params=PARAMS,
        name="finish",
    )(here, from_them, old, pos_vel, acc_jerk)


A_DEV = 128


def solution(mesh):
    in_specs = (
        P(None, ("runs", "ja")),
        P(None, ("runs", "ja")),
        P(("runs", "ja")),
        P(("runs", "ja")),
        P(("runs", "ja")),
        P(("runs", "ja")),
        P(("runs", "ja"), None),
    )
    out_specs = (P(None, ("runs", "ja")), P(None, ("runs", "ja")), P(None, ("runs", "ja")))
    return jax.shard_map(
        functools.partial(per_device, mesh.shape["ja"], 2 * A_DEV),
        mesh=mesh,
        in_specs=in_specs,
        out_specs=out_specs,
        check_vma=False,
    )
```

```python
import functools

import jax
import jax.numpy as jnp
from jax import lax
from jax.experimental import pallas as pl
from jax.experimental.pallas import tpu as pltpu
from jax.sharding import PartitionSpec as P

soft_sq = 0.01
base_step = 2.0
f32 = jnp.float32
bf16 = jnp.bfloat16

CHUNK = 128
TOGETHER = 4
FACTOR_ROWS = 128
PARAMS = pltpu.CompilerParams(vmem_limit_bytes=32 << 20)


def round_bf16(values):
    return values.astype(bf16).astype(f32)


def split(values, terms):
    out = []
    for _ in range(terms - 1):
        head = round_bf16(values)
        out.append(head)
        values = values - head
    return out + [round_bf16(values)]


def four_terms(state):
    grid = jnp.floor(state * 4.0 + 0.5) * 0.25
    low = state - grid
    low1, low2, low3 = split(low, 3)
    return grid, low1, low2, low3, low


def row_index(state):
    return lax.broadcasted_iota(jnp.int32, state.shape, 0)


def down3(state):
    return jnp.concatenate([state[5:8], state[0:5]], axis=0)


def source_factors(state):
    row = row_index(state)
    grid, low1, low2, low3, low = four_terms(state)
    square = jnp.where(row == 6, 1.0, grid * grid)
    rest = jnp.where(row < 3, (2.0 * grid + low) * low, (grid + low) * down3(grid + low))
    rest1, rest2, rest3 = [jnp.where(row == 6, 1.0, term) for term in split(rest, 3)]
    square1 = round_bf16(square)
    square2 = jnp.where(row == 6, 1.0, square - square1)
    groups = [grid, square1, square2, grid, grid, grid, low1, low1, low1, low2, low2, low3, rest1, rest2, rest3]
    pad = [jnp.zeros_like(state)] * (FACTOR_ROWS // 8 - len(groups))
    return jnp.concatenate(groups + pad, axis=0).astype(bf16)


def target_factors(state):
    grid, low1, low2, low3, low = four_terms(state)
    zero, one = jnp.zeros_like(state), jnp.ones_like(state)
    z1, z2, z3 = zero[0:1], zero[0:2], zero[0:3]

    def add3(values):
        return values[0:1] + values[1:2] + values[2:3]

    def near(values):
        return jnp.concatenate([-2.0 * values[0:3], z3, z2], axis=0)

    def crossed(values):
        return jnp.concatenate([-values[3:6], -values[0:3], z2], axis=0)

    def sums(first, second, scalar):
        return jnp.concatenate([first, second, scalar, z1], axis=0)

    square1, square2 = split(add3(grid[0:3] * grid[0:3]), 2)
    rest = split(add3((2.0 * grid[0:3] + low[0:3]) * low[0:3]) + soft_sq, 3)
    moved = split(add3((grid + low)[0:3] * (grid + low)[3:6]), 3)
    o3 = one[0:3]
    dist = [near(grid), sums(o3, z3, square1), sums(o3, z3, square2), near(low1), near(low2), near(low3)]
    dist += [near(grid), near(low1), near(low2), near(grid), near(low1), near(grid)]
    dist += [sums(o3, z3, term) for term in rest]
    radial = [crossed(grid), zero, zero, crossed(low1), crossed(low2), crossed(low3)]
    radial += [crossed(grid), crossed(low1), crossed(low2), crossed(grid), crossed(low1), crossed(grid)]
    radial += [sums(z3, o3, term) for term in moved]
    pad = [zero] * (FACTOR_ROWS // 8 - len(dist))
    return jnp.concatenate(
        [jnp.concatenate(radial + pad, axis=0), jnp.concatenate(dist + pad, axis=0)], axis=1
    ).astype(bf16)


def sum_factors(state):
    row = row_index(state)
    mass = jnp.broadcast_to(state[6:7], state.shape)
    by_weight = mass * jnp.where(row < 6, state, jnp.where(row == 6, 1.0, 0.0))
    by_radial = mass * jnp.where(row < 3, 0.0, jnp.where(row < 6, -3.0 * down3(state), jnp.where(row == 7, 3.0, 0.0)))
    return (
        jnp.concatenate(split(by_weight, 3), axis=0).astype(bf16),
        jnp.concatenate(split(by_radial, 3), axis=0).astype(bf16),
    )


def pair_weights(products):
    sources, slots = products.shape[0], products.shape[1] // 2
    parts = [[], [], [], []]
    for g in range(0, sources, 16):
        rows = [[], [], [], []]
        for lane in range(0, slots, 128):
            radial = products[g : g + 16, lane : lane + 128]
            dist_sq = products[g : g + 16, slots + lane : slots + lane + 128]
            inverse = lax.rsqrt(dist_sq)
            inverse_sq = inverse * inverse
            weight = inverse * inverse_sq
            radial = weight * (inverse_sq * radial)
            weight_hi, radial_hi = weight.astype(bf16), radial.astype(bf16)
            rows[0].append(weight_hi)
            rows[1].append((weight - weight_hi.astype(f32)).astype(bf16))
            rows[2].append(radial_hi)
            rows[3].append((radial - radial_hi.astype(f32)).astype(bf16))
        for part, row in zip(parts, rows):
            part.append(jnp.concatenate(row, axis=1))
    return jnp.concatenate(parts[0] + parts[1] + parts[2] + parts[3], axis=0)


def add_pairs(states, factors, sums):
    for state in states:
        factors_s = source_factors(state).T
        by_weight, by_radial = sum_factors(state)
        for at in range(0, state.shape[1], CHUNK):
            span = slice(at, at + CHUNK)
            left = jnp.concatenate([by_weight[:, span]] * 2 + [by_radial[:, span]] * 2, axis=1)
            for factors_t, out in zip(factors, sums):
                products = jnp.dot(factors_s[span], factors_t, preferred_element_type=f32)
                out[...] += jnp.dot(left, pair_weights(products), preferred_element_type=f32)


def add_blocks(sources, factors, sums):
    counts = [ref.shape[0] // 8 for ref in sources]
    if sum(counts) <= TOGETHER:
        rows = [ref[b : b + 8] for ref in sources for b in range(0, ref.shape[0], 8)]
        add_pairs(rows, factors, sums)
        return
    together = next(t for t in range(TOGETHER, 0, -1) if all(c % t == 0 for c in counts))
    for ref, count in zip(sources, counts):

        def step(i, _):
            rows = [ref[pl.ds(pl.multiple_of((i * together + b) * 8, 8), 8), :] for b in range(together)]
            add_pairs(rows, factors, sums)
            return 0

        lax.fori_loop(0, count // together, step, 0)


def one_hot(order, stars):
    row = lax.broadcasted_iota(jnp.int32, (stars, order.shape[1]), 0)
    return jnp.where(row == order, 1.0, 0.0).astype(f32).astype(bf16)


def spread(hot, live):
    rows = jnp.broadcast_to(live, (16, live.shape[1])).astype(bf16)
    return lax.dot_general(rows, hot, (((1,), (1,)), ((), ())), preferred_element_type=f32)[0:1]


def exact_product(rows, hot, contract):
    height = rows.shape[0]
    terms = jnp.concatenate(split(rows, 3), axis=0).astype(bf16)
    out = lax.dot_general(terms, hot, (((1,), (contract,)), ((), ())), preferred_element_type=f32)
    return out[0:height] + out[height : 2 * height] + out[2 * height : 3 * height]


def prepare_kernel(slots, *refs):
    inputs, (src_ref, tgt_ref, old_ref, fac_ref), here, sems = refs[:7], refs[7:11], refs[11:18], refs[18]
    copies = [pltpu.make_async_copy(src, dst, sems.at[i]) for i, (src, dst) in enumerate(zip(inputs, here))]
    for copy in copies:
        copy.start()
    pv_ref, aj_ref, mass_ref, phase_ref, level_ref, count_ref, order_ref = here
    stars = pv_ref.shape[1]
    copies[5].wait()
    copies[6].wait()
    order = order_ref[0:1, 0:slots]
    hot = one_hot(order, stars)
    live = jnp.where(lax.broadcasted_iota(jnp.int32, (1, slots), 1) < count_ref[...], 1.0, 0.0)
    active = spread(hot, live)
    for copy in copies[:5]:
        copy.wait()
    level = level_ref[...]
    step_len = base_step * jnp.where((level & 1) > 0, 0.5, 1.0) * jnp.where((level & 2) > 0, 0.25, 1.0)
    age = step_len * jnp.where(active > 0.5, 1.0, phase_ref[...])
    half_sq = 0.5 * age * age
    sixth_cube = age * age * age / 6.0
    pv, aj = pv_ref[...], aj_ref[...]
    x, v, a, j = pv[0:3], pv[3:6], aj[0:3], aj[3:6]
    position = x + age * v + half_sq * a + sixth_cube * j
    velocity = v + age * a + half_sq * j
    state = jnp.concatenate([position, velocity, mass_ref[...], step_len], axis=0)
    src_ref[...] = state
    gap = jnp.zeros((2, stars), f32)
    old = exact_product(jnp.concatenate([state, pv, gap, aj, gap], axis=0), hot, 0)
    tgt_ref[...] = old[0:8]
    old_ref[...] = jnp.concatenate([old[0:22], live, order.astype(f32)], axis=0)
    fac_ref[...] = target_factors(old[0:8])


def first_kernel(src_ref, mine_ref, theirs_ref, out_mine, out_theirs, fac_ref):
    factors = target_factors(theirs_ref[...])
    fac_ref[...] = factors
    for out in (out_mine, out_theirs):
        out[...] = jnp.zeros_like(out)
    add_blocks([src_ref], [mine_ref[...], factors], [out_mine, out_theirs])


def pair_kernel(parts, sets, folded, *refs):
    sources, refs = refs[:parts], refs[parts:]
    factors, sums_in, outs, rest = refs[:sets], refs[sets : 2 * sets], refs[2 * sets : 3 * sets], refs[3 * sets :]
    if folded:
        outs, folded_outs = rest, outs
    for out, sums in zip(outs, sums_in):
        out[...] = sums[...]
    add_blocks(sources, [ref[...] for ref in factors], outs)
    if folded:
        for out, sums in zip(folded_outs, outs):
            out[...] = sums[0:8] + sums[8:16] + sums[16:24]


def finish_kernel(mine_ref, other_ref, old_ref, pv_ref, aj_ref, new_pv_ref, new_aj_ref, state_ref):
    stars = pv_ref.shape[1]
    sums = mine_ref[...] + other_ref[...]
    old = old_ref[...]
    here, there, step_len = old[0:3], old[3:6], old[7:8]
    a1 = sums[0:3] - here * sums[6:7]
    j1 = sums[3:6] - there * sums[6:7] + here * sums[7:8]
    x0, v0, a0, j0 = old[8:11], old[11:14], old[16:19], old[19:22]
    half_step = 0.5 * step_len
    twelfth = step_len * step_len / 12.0
    v1 = v0 + half_step * (a0 + a1) + twelfth * (j0 - j1)
    x1 = x0 + half_step * (v0 + v1) + twelfth * (a0 - a1)
    live = old[22:23]
    state = jnp.where(live > 0.5, jnp.concatenate([x1, v1, a1, j1], axis=0), 0.0)
    state_ref[...] = state
    hot = one_hot(old[23:24].astype(jnp.int32), stars)
    rows = jnp.concatenate([state, jnp.broadcast_to(live, (4, live.shape[1]))], axis=0)
    moved = exact_product(rows, hot, 1)
    active = moved[12:13] > 0.5
    new_pv_ref[...] = jnp.where(active, moved[0:6], pv_ref[...])
    new_aj_ref[...] = jnp.where(active, moved[6:12], aj_ref[...])


VMEM = pl.BlockSpec(memory_space=pltpu.VMEM)
HBM = pl.BlockSpec(memory_space=pltpu.HBM)


def cost(sources, slots):
    pairs = sum(s.size // 8 for s in sources) * slots
    return pl.CostEstimate(flops=3072 * pairs, bytes_accessed=4 * pairs // slots, transcendentals=pairs)


def call_pairs(sources, factors, sums, folded=False):
    sets, slots = len(factors), factors[0].shape[1] // 2
    operands = list(sources) + list(factors) + list(sums)
    shape = (24, slots)
    return pl.pallas_call(
        functools.partial(pair_kernel, len(sources), sets, folded),
        out_shape=(jax.ShapeDtypeStruct((8, slots) if folded else shape, f32),) * sets,
        in_specs=[VMEM] * len(operands),
        out_specs=(VMEM,) * sets,
        scratch_shapes=[pltpu.VMEM(shape, f32)] * (sets if folded else 0),
        compiler_params=PARAMS,
        cost_estimate=cost(sources, sets * slots),
        name="pairs",
    )(*operands)


def per_device(n, slots, pos_vel, acc_jerk, star_mass, step_phase, step_level, counts, star_order):
    stars = pos_vel.shape[1]
    inputs = [pos_vel, acc_jerk] + [values.reshape(1, -1) for values in (star_mass, step_phase, step_level, counts)]
    inputs.append(star_order)
    factor_shape = jax.ShapeDtypeStruct((FACTOR_ROWS, 2 * slots), bf16)
    own, targets, old, mine = pl.pallas_call(
        functools.partial(prepare_kernel, slots),
        out_shape=(
            jax.ShapeDtypeStruct((8, stars), f32),
            jax.ShapeDtypeStruct((8, slots), f32),
            jax.ShapeDtypeStruct((24, slots), f32),
            factor_shape,
        ),
        in_specs=[HBM] * 7,
        out_specs=(VMEM,) * 4,
        scratch_shapes=[pltpu.VMEM(values.shape, values.dtype) for values in inputs] + [pltpu.SemaphoreType.DMA((7,))],
        compiler_params=PARAMS,
        name="prepare",
    )(*[pltpu.with_memory_space_constraint(values, pltpu.HBM) if values.size > 1 else values for values in inputs])

    def swap(values, bit):
        return lax.ppermute(values, "ja", [(i, i ^ bit) for i in range(n)])

    def after(sums, *values):
        *values, first, second = lax.optimization_barrier(values + tuple(sums))
        return *values, (first, second)

    theirs = swap(targets, 1)
    held, bit = own, n // 2
    near = swap(held, 2) if bit == 8 else None
    coming = swap(held, bit)
    *sums, theirs = pl.pallas_call(
        first_kernel,
        out_shape=(jax.ShapeDtypeStruct((24, slots), f32),) * 2 + (factor_shape,),
        in_specs=[VMEM] * 3,
        out_specs=(VMEM,) * 3,
        compiler_params=PARAMS,
        cost_estimate=cost([own], 2 * slots),
        name="first",
    )(own, mine, theirs)
    both = (mine, theirs)
    while bit > 8:
        arrived, sums = after(sums, coming)
        held = jnp.concatenate([held, arrived], axis=0)
        bit //= 2
        near = swap(held, 2) if bit == 8 else None
        coming = swap(held, bit)
        sums = call_pairs([arrived], both, sums)
    arrived, sums = after(sums, coming)
    beside = swap(jnp.concatenate([held, arrived], axis=0), 4)
    coming = swap(arrived, 2)
    near, sums = after(sums, near)
    sums = call_pairs([arrived, near], both, sums)
    arrived, sums = after(sums, coming)
    coming = swap(jnp.concatenate([near, arrived], axis=0), 4)
    beside, sums = after(sums, beside)
    sums = call_pairs([arrived, beside], both, sums)
    last, sums = after(sums, coming)
    (for_them,) = call_pairs([last], [theirs], [sums[1]], folded=True)
    from_them = swap(for_them, 1)
    (here,) = call_pairs([last], [mine], [sums[0]], folded=True)
    return pl.pallas_call(
        finish_kernel,
        out_shape=(
            jax.ShapeDtypeStruct(pos_vel.shape, f32),
            jax.ShapeDtypeStruct(acc_jerk.shape, f32),
            jax.ShapeDtypeStruct((12, slots), f32),
        ),
        in_specs=[VMEM] * 5,
        out_specs=(VMEM,) * 3,
        compiler_params=PARAMS,
        name="finish",
    )(here, from_them, old, pos_vel, acc_jerk)


A_DEV = 128


def solution(mesh):
    in_specs = (
        P(None, ("runs", "ja")),
        P(None, ("runs", "ja")),
        P(("runs", "ja")),
        P(("runs", "ja")),
        P(("runs", "ja")),
        P(("runs", "ja")),
        P(("runs", "ja"), None),
    )
    out_specs = (P(None, ("runs", "ja")), P(None, ("runs", "ja")), P(None, ("runs", "ja")))
    return jax.shard_map(
        functools.partial(per_device, mesh.shape["ja"], 2 * A_DEV),
        mesh=mesh,
        in_specs=in_specs,
        out_specs=out_specs,
        check_vma=False,
    )
```

```python
import functools

import jax
import jax.numpy as jnp
from jax import lax
from jax.experimental import pallas as pl
from jax.experimental.pallas import tpu as pltpu
from jax.sharding import PartitionSpec as P

soft_sq = 0.01
base_step = 2.0
f32 = jnp.float32
bf16 = jnp.bfloat16

CHUNK = 128
TOGETHER = 4
FACTOR_ROWS = 128
PARAMS = pltpu.CompilerParams(vmem_limit_bytes=32 << 20)


def round_bf16(values):
    return values.astype(bf16).astype(f32)


def split(values, terms):
    out = []
    for _ in range(terms - 1):
        head = round_bf16(values)
        out.append(head)
        values = values - head
    return out + [round_bf16(values)]


def four_terms(state):
    grid = jnp.floor(state * 4.0 + 0.5) * 0.25
    low = state - grid
    low1, low2, low3 = split(low, 3)
    return grid, low1, low2, low3, low


def row_index(state):
    return lax.broadcasted_iota(jnp.int32, state.shape, 0)


def down3(state):
    return jnp.concatenate([state[5:8], state[0:5]], axis=0)


def source_factors(state):
    row = row_index(state)
    grid, low1, low2, low3, low = four_terms(state)
    square = jnp.where(row == 6, 1.0, grid * grid)
    rest = jnp.where(row < 3, (2.0 * grid + low) * low, (grid + low) * down3(grid + low))
    rest1, rest2, rest3 = [jnp.where(row == 6, 1.0, term) for term in split(rest, 3)]
    square1 = round_bf16(square)
    square2 = jnp.where(row == 6, 1.0, square - square1)
    groups = [grid, square1, square2, grid, grid, grid, low1, low1, low1, low2, low2, low3, rest1, rest2, rest3]
    pad = [jnp.zeros_like(state)] * (FACTOR_ROWS // 8 - len(groups))
    return jnp.concatenate(groups + pad, axis=0).astype(bf16)


def target_factors(state):
    grid, low1, low2, low3, low = four_terms(state)
    zero, one = jnp.zeros_like(state), jnp.ones_like(state)
    z1, z2, z3 = zero[0:1], zero[0:2], zero[0:3]

    def add3(values):
        return values[0:1] + values[1:2] + values[2:3]

    def near(values):
        return jnp.concatenate([-2.0 * values[0:3], z3, z2], axis=0)

    def crossed(values):
        return jnp.concatenate([-values[3:6], -values[0:3], z2], axis=0)

    def sums(first, second, scalar):
        return jnp.concatenate([first, second, scalar, z1], axis=0)

    square1, square2 = split(add3(grid[0:3] * grid[0:3]), 2)
    rest = split(add3((2.0 * grid[0:3] + low[0:3]) * low[0:3]) + soft_sq, 3)
    moved = split(add3((grid + low)[0:3] * (grid + low)[3:6]), 3)
    o3 = one[0:3]
    dist = [near(grid), sums(o3, z3, square1), sums(o3, z3, square2), near(low1), near(low2), near(low3)]
    dist += [near(grid), near(low1), near(low2), near(grid), near(low1), near(grid)]
    dist += [sums(o3, z3, term) for term in rest]
    radial = [crossed(grid), zero, zero, crossed(low1), crossed(low2), crossed(low3)]
    radial += [crossed(grid), crossed(low1), crossed(low2), crossed(grid), crossed(low1), crossed(grid)]
    radial += [sums(z3, o3, term) for term in moved]
    pad = [zero] * (FACTOR_ROWS // 8 - len(dist))
    return jnp.concatenate(
        [jnp.concatenate(radial + pad, axis=0), jnp.concatenate(dist + pad, axis=0)], axis=1
    ).astype(bf16)


def sum_factors(state):
    row = row_index(state)
    mass = jnp.broadcast_to(state[6:7], state.shape)
    by_weight = mass * jnp.where(row < 6, state, jnp.where(row == 6, 1.0, 0.0))
    by_radial = mass * jnp.where(row < 3, 0.0, jnp.where(row < 6, -3.0 * down3(state), jnp.where(row == 7, 3.0, 0.0)))
    return (
        jnp.concatenate(split(by_weight, 3), axis=0).astype(bf16),
        jnp.concatenate(split(by_radial, 3), axis=0).astype(bf16),
    )


def pair_weights(products):
    sources, slots = products.shape[0], products.shape[1] // 2
    parts = [[], [], [], []]
    for g in range(0, sources, 16):
        rows = [[], [], [], []]
        for lane in range(0, slots, 128):
            radial = products[g : g + 16, lane : lane + 128]
            dist_sq = products[g : g + 16, slots + lane : slots + lane + 128]
            inverse = lax.rsqrt(dist_sq)
            inverse_sq = inverse * inverse
            weight = inverse * inverse_sq
            radial = weight * (inverse_sq * radial)
            weight_hi, radial_hi = weight.astype(bf16), radial.astype(bf16)
            rows[0].append(weight_hi)
            rows[1].append((weight - weight_hi.astype(f32)).astype(bf16))
            rows[2].append(radial_hi)
            rows[3].append((radial - radial_hi.astype(f32)).astype(bf16))
        for part, row in zip(parts, rows):
            part.append(jnp.concatenate(row, axis=1))
    return jnp.concatenate(parts[0] + parts[1] + parts[2] + parts[3], axis=0)


def add_pairs(states, factors, sums):
    for state in states:
        factors_s = source_factors(state).T
        by_weight, by_radial = sum_factors(state)
        for at in range(0, state.shape[1], CHUNK):
            span = slice(at, at + CHUNK)
            left = jnp.concatenate([by_weight[:, span]] * 2 + [by_radial[:, span]] * 2, axis=1)
            for factors_t, out in zip(factors, sums):
                products = jnp.dot(factors_s[span], factors_t, preferred_element_type=f32)
                out[...] += jnp.dot(left, pair_weights(products), preferred_element_type=f32)


def add_blocks(sources, factors, sums):
    counts = [ref.shape[0] // 8 for ref in sources]
    if sum(counts) <= TOGETHER:
        rows = [ref[b : b + 8] for ref in sources for b in range(0, ref.shape[0], 8)]
        add_pairs(rows, factors, sums)
        return
    together = next(t for t in range(TOGETHER, 0, -1) if all(c % t == 0 for c in counts))
    for ref, count in zip(sources, counts):

        def step(i, _):
            rows = [ref[pl.ds(pl.multiple_of((i * together + b) * 8, 8), 8), :] for b in range(together)]
            add_pairs(rows, factors, sums)
            return 0

        lax.fori_loop(0, count // together, step, 0)


def one_hot(order, stars):
    row = lax.broadcasted_iota(jnp.int32, (stars, order.shape[1]), 0)
    return jnp.where(row == order, 1.0, 0.0).astype(f32).astype(bf16)


def spread(hot, live):
    rows = jnp.broadcast_to(live, (16, live.shape[1])).astype(bf16)
    return lax.dot_general(rows, hot, (((1,), (1,)), ((), ())), preferred_element_type=f32)[0:1]


def exact_product(rows, hot, contract):
    height = rows.shape[0]
    terms = jnp.concatenate(split(rows, 3), axis=0).astype(bf16)
    out = lax.dot_general(terms, hot, (((1,), (contract,)), ((), ())), preferred_element_type=f32)
    return out[0:height] + out[height : 2 * height] + out[2 * height : 3 * height]


def prepare_kernel(slots, *refs):
    inputs, (src_ref, tgt_ref, old_ref, fac_ref, turned_ref), here, sems = refs[:7], refs[7:12], refs[12:19], refs[19]
    copies = [pltpu.make_async_copy(src, dst, sems.at[i]) for i, (src, dst) in enumerate(zip(inputs, here))]
    for copy in copies:
        copy.start()
    pv_ref, aj_ref, mass_ref, phase_ref, level_ref, count_ref, order_ref = here
    stars = pv_ref.shape[1]
    copies[5].wait()
    copies[6].wait()
    order = order_ref[0:1, 0:slots]
    hot = one_hot(order, stars)
    live = jnp.where(lax.broadcasted_iota(jnp.int32, (1, slots), 1) < count_ref[...], 1.0, 0.0)
    active = spread(hot, live)
    for copy in copies[:5]:
        copy.wait()
    level = level_ref[...]
    step_len = base_step * jnp.where((level & 1) > 0, 0.5, 1.0) * jnp.where((level & 2) > 0, 0.25, 1.0)
    age = step_len * jnp.where(active > 0.5, 1.0, phase_ref[...])
    half_sq = 0.5 * age * age
    sixth_cube = age * age * age / 6.0
    pv, aj = pv_ref[...], aj_ref[...]
    x, v, a, j = pv[0:3], pv[3:6], aj[0:3], aj[3:6]
    position = x + age * v + half_sq * a + sixth_cube * j
    velocity = v + age * a + half_sq * j
    state = jnp.concatenate([position, velocity, mass_ref[...], step_len], axis=0)
    src_ref[...] = state
    gap = jnp.zeros((2, stars), f32)
    old = exact_product(jnp.concatenate([state, pv, gap, aj, gap], axis=0), hot, 0)
    tgt_ref[...] = old[0:8]
    old_ref[...] = jnp.concatenate([old[0:22], live, order.astype(f32)], axis=0)
    fac_ref[...] = target_factors(old[0:8])
    turned_ref[...] = hot.T


def first_kernel(src_ref, mine_ref, theirs_ref, out_mine, out_theirs, fac_ref):
    factors = target_factors(theirs_ref[...])
    fac_ref[...] = factors
    for out in (out_mine, out_theirs):
        out[...] = jnp.zeros_like(out)
    add_blocks([src_ref], [mine_ref[...], factors], [out_mine, out_theirs])


def pair_kernel(parts, sets, folded, *refs):
    sources, refs = refs[:parts], refs[parts:]
    factors, sums_in, outs, rest = refs[:sets], refs[sets : 2 * sets], refs[2 * sets : 3 * sets], refs[3 * sets :]
    if folded:
        outs, folded_outs = rest, outs
    for out, sums in zip(outs, sums_in):
        out[...] = sums[...]
    add_blocks(sources, [ref[...] for ref in factors], outs)
    if folded:
        for out, sums in zip(folded_outs, outs):
            out[...] = sums[0:8] + sums[8:16] + sums[16:24]


def finish_kernel(mine_ref, other_ref, turned_ref, old_ref, pv_ref, aj_ref, new_pv_ref, new_aj_ref, state_ref):
    sums = mine_ref[...] + other_ref[...]
    old = old_ref[...]
    here, there, step_len = old[0:3], old[3:6], old[7:8]
    a1 = sums[0:3] - here * sums[6:7]
    j1 = sums[3:6] - there * sums[6:7] + here * sums[7:8]
    x0, v0, a0, j0 = old[8:11], old[11:14], old[16:19], old[19:22]
    half_step = 0.5 * step_len
    twelfth = step_len * step_len / 12.0
    v1 = v0 + half_step * (a0 + a1) + twelfth * (j0 - j1)
    x1 = x0 + half_step * (v0 + v1) + twelfth * (a0 - a1)
    live = old[22:23]
    state = jnp.where(live > 0.5, jnp.concatenate([x1, v1, a1, j1], axis=0), 0.0)
    state_ref[...] = state
    rows = jnp.concatenate([state, jnp.broadcast_to(live, (4, live.shape[1]))], axis=0)
    moved = exact_product(rows, turned_ref[...], 0)
    active = moved[12:13] > 0.5
    new_pv_ref[...] = jnp.where(active, moved[0:6], pv_ref[...])
    new_aj_ref[...] = jnp.where(active, moved[6:12], aj_ref[...])


VMEM = pl.BlockSpec(memory_space=pltpu.VMEM)
HBM = pl.BlockSpec(memory_space=pltpu.HBM)


def cost(sources, slots):
    pairs = sum(s.size // 8 for s in sources) * slots
    return pl.CostEstimate(flops=3072 * pairs, bytes_accessed=4 * pairs // slots, transcendentals=pairs)


def call_pairs(sources, factors, sums, folded=False):
    sets, slots = len(factors), factors[0].shape[1] // 2
    operands = list(sources) + list(factors) + list(sums)
    shape = (24, slots)
    return pl.pallas_call(
        functools.partial(pair_kernel, len(sources), sets, folded),
        out_shape=(jax.ShapeDtypeStruct((8, slots) if folded else shape, f32),) * sets,
        in_specs=[VMEM] * len(operands),
        out_specs=(VMEM,) * sets,
        scratch_shapes=[pltpu.VMEM(shape, f32)] * (sets if folded else 0),
        compiler_params=PARAMS,
        cost_estimate=cost(sources, sets * slots),
        name="pairs",
    )(*operands)


def per_device(n, slots, pos_vel, acc_jerk, star_mass, step_phase, step_level, counts, star_order):
    stars = pos_vel.shape[1]
    inputs = [pos_vel, acc_jerk] + [values.reshape(1, -1) for values in (star_mass, step_phase, step_level, counts)]
    inputs.append(star_order)
    factor_shape = jax.ShapeDtypeStruct((FACTOR_ROWS, 2 * slots), bf16)
    own, targets, old, mine, turned = pl.pallas_call(
        functools.partial(prepare_kernel, slots),
        out_shape=(
            jax.ShapeDtypeStruct((8, stars), f32),
            jax.ShapeDtypeStruct((8, slots), f32),
            jax.ShapeDtypeStruct((24, slots), f32),
            factor_shape,
            jax.ShapeDtypeStruct((slots, stars), bf16),
        ),
        in_specs=[HBM] * 7,
        out_specs=(VMEM,) * 5,
        scratch_shapes=[pltpu.VMEM(values.shape, values.dtype) for values in inputs] + [pltpu.SemaphoreType.DMA((7,))],
        compiler_params=PARAMS,
        name="prepare",
    )(*[pltpu.with_memory_space_constraint(values, pltpu.HBM) if values.size > 1 else values for values in inputs])

    def swap(values, bit):
        return lax.ppermute(values, "ja", [(i, i ^ bit) for i in range(n)])

    def after(sums, *values):
        *values, first, second = lax.optimization_barrier(values + tuple(sums))
        return *values, (first, second)

    theirs = swap(targets, 1)
    held, bit = own, n // 2
    near = swap(held, 2) if bit == 8 else None
    coming = swap(held, bit)
    *sums, theirs = pl.pallas_call(
        first_kernel,
        out_shape=(jax.ShapeDtypeStruct((24, slots), f32),) * 2 + (factor_shape,),
        in_specs=[VMEM] * 3,
        out_specs=(VMEM,) * 3,
        compiler_params=PARAMS,
        cost_estimate=cost([own], 2 * slots),
        name="first",
    )(own, mine, theirs)
    both = (mine, theirs)
    while bit > 8:
        arrived, sums = after(sums, coming)
        held = jnp.concatenate([held, arrived], axis=0)
        bit //= 2
        near = swap(held, 2) if bit == 8 else None
        coming = swap(held, bit)
        sums = call_pairs([arrived], both, sums)
    arrived, sums = after(sums, coming)
    beside = swap(jnp.concatenate([held, arrived], axis=0), 4)
    coming = swap(arrived, 2)
    near, sums = after(sums, near)
    sums = call_pairs([arrived, near], both, sums)
    arrived, sums = after(sums, coming)
    coming = swap(jnp.concatenate([near, arrived], axis=0), 4)
    beside, sums = after(sums, beside)
    sums = call_pairs([arrived, beside], both, sums)
    last, sums = after(sums, coming)
    (for_them,) = call_pairs([last], [theirs], [sums[1]], folded=True)
    from_them = swap(for_them, 1)
    (here,) = call_pairs([last], [mine], [sums[0]], folded=True)
    return pl.pallas_call(
        finish_kernel,
        out_shape=(
            jax.ShapeDtypeStruct(pos_vel.shape, f32),
            jax.ShapeDtypeStruct(acc_jerk.shape, f32),
            jax.ShapeDtypeStruct((12, slots), f32),
        ),
        in_specs=[VMEM] * 6,
        out_specs=(VMEM,) * 3,
        compiler_params=PARAMS,
        name="finish",
    )(here, from_them, turned, old, pos_vel, acc_jerk)


A_DEV = 128


def solution(mesh):
    in_specs = (
        P(None, ("runs", "ja")),
        P(None, ("runs", "ja")),
        P(("runs", "ja")),
        P(("runs", "ja")),
        P(("runs", "ja")),
        P(("runs", "ja")),
        P(("runs", "ja"), None),
    )
    out_specs = (P(None, ("runs", "ja")), P(None, ("runs", "ja")), P(None, ("runs", "ja")))
    return jax.shard_map(
        functools.partial(per_device, mesh.shape["ja"], 2 * A_DEV),
        mesh=mesh,
        in_specs=in_specs,
        out_specs=out_specs,
        check_vma=False,
    )
```
